512 devices in a mesh: gx: 16 (over y, core), gy: 32 (over z, x).
Axes of the slice: x: 4, y: 8, z: 8, core: 2. Of those that a mesh axis runs over, the one named last changes fastest.
Arguments:
- layer_input: bfloat16 [20, 128, 128, 1024], P(None, 'gx', 'gy'), may hold values from -6 to 6
- cotangent: bfloat16 [20, 128, 128, 1024], P(None, 'gx', 'gy'), may hold values from -6 to 6
- log_perm: float32 [128, 128, 64], P('gx', 'gy'), may hold values from -6 to 6
- well_cells: int32 [32], replicated, may hold values from 0 to 16383
- well_rates: int32 [32, 16], replicated, may hold values from 0 to 8
- inject_gain: float32 [2, 20], replicated, may hold values from -4 to 4
- spectral_weight: bfloat16 [2, 576, 144, 400], P(None, 'gy', 'gx'), may hold values from -12 to 12
- point_weight: bfloat16 [20, 20], replicated, may hold values from -1.25 to 1.25
- point_bias: float32 [20], replicated, may hold values from -3 to 3
Outputs:
- grad_input: bfloat16 [20, 128, 128, 1024], P(None, 'gx', 'gy')
- grad_spectral: float32 [2, 576, 144, 400], P(None, 'gy', 'gx')
- grad_perm: float32 [128, 128, 64], P('gx', 'gy')
The draws below stay inside these ranges and needn't reach their ends.
Inputs may be any that keep to these rules, and one draw needn't show every extreme that they name: `well_cells`: several wells may share a column.
All inputs are finite; a program needn't handle non-finite values.
Results may differ from the reference program's by a relative error of at most 0.035.
Values may be sent and summed in bfloat16 or wider, within the bound.
A program may use at most 128 MiB of HBM per device.

```python
import math
import jax
import jax.numpy as jnp
from jax import lax

C = 20
NX = 128
NY = 128
NZ = 64
NT = 16
MX = 24
MY = 24
MZ = 24
MT = 6
NW = 32
MXY = 576
MZT = 144
ZT = 1024


def touch_ends(drawn, stream_key, smallest, high):
    extent = drawn.shape
    index_at = [jax.random.randint(jax.random.fold_in(stream_key, axis), (), 0, extent[axis]) for axis in range(len(extent))]
    drawn = drawn.at[tuple(index_at)].set(smallest)
    longest = extent.index(max(extent))
    index_at[longest] = (index_at[longest] + 1) % extent[longest]
    return drawn.at[tuple(index_at)].set(high)


def block_scale(stream_key, extent, cuts, low, high):
    def one(dim, shards_of):
        heights = jax.random.uniform(jax.random.fold_in(jax.random.fold_in(stream_key, 6), dim), (shards_of,), jnp.float32, low / len(cuts), high / len(cuts))
        return jnp.repeat(jnp.exp(heights), extent[dim] // shards_of).reshape((-1,) + (1,) * (len(extent) - dim - 1))

    factor_of = one(*cuts[0])
    for cut in cuts[1:]:
        factor_of = factor_of * one(*cut)
    return factor_of


def normal_values(stream_key, dims, deviation, bound, cuts=(), kind=jnp.bfloat16):
    level = block_scale(stream_key, dims, cuts, -0.22, 0.18) if cuts else 1.0
    array = jax.random.normal(stream_key, dims, jnp.float32) * deviation * level
    return jnp.minimum(jnp.maximum(array, -bound), bound).astype(kind)


def setup_inputs(seed: int = 0) -> dict:
    seeds = jax.random.split(jax.random.key(seed), 10)
    return {
        "layer_input": normal_values(seeds[0], (C, NX, NY, ZT), 1.0, 6.0, ((1, 16), (2, 32))),
        "cotangent": normal_values(seeds[1], (C, NX, NY, ZT), 1.0, 6.0, ((1, 16), (2, 32))),
        "log_perm": normal_values(seeds[2], (NX, NY, NZ), 1.0, 6.0, ((0, 16), (1, 32)), jnp.float32),
        "well_cells": touch_ends(jax.random.randint(seeds[3], (NW,), 0, NX * NY), jax.random.fold_in(seeds[3], 1), 0, (NX * NY) - 1).astype(jnp.int32),
        "well_rates": touch_ends(jax.random.randint(seeds[4], (NW, NT), 0, 9), jax.random.fold_in(seeds[4], 1), 0, 8).astype(jnp.int32),
        "inject_gain": normal_values(seeds[5], (2, C), 0.25, 4.0, (), jnp.float32),
        "spectral_weight": normal_values(seeds[6], (2, MXY, MZT, C * C), 2.0, 12.0, ((1, 32), (2, 16))),
        "point_weight": normal_values(seeds[7], (C, C), C ** -0.5, 1.25),
        "point_bias": normal_values(seeds[8], (C,), 0.5, 3.0, (), jnp.float32),
    }


RATE_SCALE = 0.5
HIGH = lax.Precision.HIGHEST
INV_ROOT_TWO = 1.0 / math.sqrt(2.0)
INV_ROOT_TWO_PI = 1.0 / math.sqrt(2.0 * math.pi)

def signed_freq(index, count):
    return jnp.where(index < count // 2, index, index - count)

def wave_pair(count, length, cells):
    freq = signed_freq(jnp.arange(count, dtype=jnp.int32), count)
    turns = freq[:, None] * cells[None, :] % length
    angle = 2.0 * math.pi / length * turns.astype(jnp.float32)
    scale = 1.0 / math.sqrt(length)
    return (jnp.cos(angle) * scale, jnp.sin(angle) * scale)

def zt_tables():
    freq_z = signed_freq(jnp.arange(MZ, dtype=jnp.int32), MZ)
    freq_t = jnp.arange(MT, dtype=jnp.int32)
    depth = jnp.arange(NZ, dtype=jnp.int32)
    moment = jnp.arange(NT, dtype=jnp.int32)
    turns = (freq_z[:, None, None, None] * depth[None, None, :, None] * NT + freq_t[None, :, None, None] * moment[None, None, None, :] * NZ) % (NZ * NT)
    angle = 2.0 * math.pi / (NZ * NT) * turns.reshape(MZ * MT, NZ * NT).astype(jnp.float32)
    scale = 1.0 / math.sqrt(NZ * NT)
    cosine = jnp.cos(angle) * scale
    sine = jnp.sin(angle) * scale
    weight = jnp.tile(jnp.where(freq_t == 0, 1.0, 2.0), MZ).astype(jnp.float32)
    forward = jnp.transpose(jnp.stack([cosine, -sine]), (2, 0, 1)).astype(jnp.bfloat16)
    inverse = jnp.stack([weight[:, None] * cosine, -weight[:, None] * sine]).astype(jnp.bfloat16)
    return (forward, inverse, weight)

def narrow(value):
    return lax.optimization_barrier(value.astype(jnp.bfloat16)).astype(jnp.float32)

def gelu_slope(value):
    return 0.5 * (1.0 + lax.erf(value * INV_ROOT_TWO)) + value * jnp.exp(-0.5 * value * value) * INV_ROOT_TWO_PI

def reference(layer_input, cotangent, log_perm, well_cells, well_rates, inject_gain, spectral_weight, point_weight, point_bias):
    channels = layer_input.shape[0]
    block = math.gcd(NX, 8)
    count_blocks = NX // block
    modes_zt = MZ * MT
    modes_xy = MX * MY
    forward_zt, inverse_zt, mode_weight = zt_tables()
    forward_f = lax.optimization_barrier(forward_zt).astype(jnp.float32)
    inverse_f = lax.optimization_barrier(inverse_zt).astype(jnp.float32)
    cos_all, sin_all = wave_pair(MX, NX, jnp.arange(NX, dtype=jnp.int32))
    cos_narrow = narrow(cos_all)
    sin_narrow = narrow(sin_all)
    cos_y, sin_y = wave_pair(MY, NY, jnp.arange(NY, dtype=jnp.int32))
    cells = jnp.arange(NX * NY, dtype=jnp.int32)
    hits = (well_cells[:, None] == cells[None, :]).astype(jnp.float32)
    inflow = (RATE_SCALE * jnp.einsum('wt,wa->at', well_rates.astype(jnp.float32), hits, precision=HIGH)).reshape(NX, NY, NT)
    pw_float = point_weight.astype(jnp.float32)
    block_ids = jnp.arange(count_blocks, dtype=jnp.int32)

    def lifted_block(start):
        piece = lax.dynamic_slice_in_dim(layer_input, start, block, 1).astype(jnp.float32).reshape(channels, block, NY, NZ, NT)
        perm_piece = lax.dynamic_slice_in_dim(log_perm, start, block, 0)
        flow_piece = lax.dynamic_slice_in_dim(inflow, start, block, 0)
        total = piece + inject_gain[0][:, None, None, None, None] * perm_piece[None, :, :, :, None] + inject_gain[1][:, None, None, None, None] * flow_piece[None, :, :, None, :]
        return narrow(total).reshape(channels, block * NY, NZ * NT)

    def spectra(make_block):

        def one_block(index):
            field = make_block(index * block)
            return narrow(jnp.einsum('cak,kpm->pmca', field, forward_f, precision=HIGH))
        stacked = lax.map(one_block, block_ids)
        rows_x = jnp.moveaxis(stacked, 0, 3).reshape(2, modes_zt, channels, NX, NY)
        even = jnp.einsum('jx,pmcxy->pjmcy', cos_narrow, rows_x, precision=HIGH)
        odd = jnp.einsum('jx,pmcxy->pjmcy', sin_narrow, rows_x, precision=HIGH)
        first = even[0] + odd[1]
        second = even[1] - odd[0]
        real = jnp.einsum('ky,jmcy->jkmc', cos_y, first, precision=HIGH) + jnp.einsum('ky,jmcy->jkmc', sin_y, second, precision=HIGH)
        imag = jnp.einsum('ky,jmcy->jkmc', cos_y, second, precision=HIGH) - jnp.einsum('ky,jmcy->jkmc', sin_y, first, precision=HIGH)
        return jnp.stack([real, imag], axis=2).reshape(modes_xy, 2, modes_zt, channels)

    def field_of(spec):
        waves = spec.reshape(MX, MY, 2, modes_zt, channels)
        real = jnp.einsum('ky,jkmo->jmoy', cos_y, waves[:, :, 0], precision=HIGH) - jnp.einsum('ky,jkmo->jmoy', sin_y, waves[:, :, 1], precision=HIGH)
        imag = jnp.einsum('ky,jkmo->jmoy', cos_y, waves[:, :, 1], precision=HIGH) + jnp.einsum('ky,jkmo->jmoy', sin_y, waves[:, :, 0], precision=HIGH)
        out_re = jnp.einsum('jx,jmoy->moxy', cos_all, real, precision=HIGH) - jnp.einsum('jx,jmoy->moxy', sin_all, imag, precision=HIGH)
        out_im = jnp.einsum('jx,jmoy->moxy', cos_all, imag, precision=HIGH) + jnp.einsum('jx,jmoy->moxy', sin_all, real, precision=HIGH)
        return lax.optimization_barrier(jnp.stack([out_re, out_im]).astype(jnp.bfloat16))

    def spatial_block(image, start):
        piece = lax.dynamic_slice_in_dim(image, start, block, 3).astype(jnp.float32).reshape(2, modes_zt, channels, block * NY)
        return jnp.einsum('pmca,pmk->cak', piece, inverse_f, precision=HIGH)
    weight = spectral_weight.astype(jnp.float32).reshape(2, modes_xy, modes_zt, channels, channels)
    spec_in = spectra(lifted_block)
    mix_re = jnp.einsum('rmco,rmc->rmo', weight[0], spec_in[:, 0], precision=HIGH) - jnp.einsum('rmco,rmc->rmo', weight[1], spec_in[:, 1], precision=HIGH)
    mix_im = jnp.einsum('rmco,rmc->rmo', weight[0], spec_in[:, 1], precision=HIGH) + jnp.einsum('rmco,rmc->rmo', weight[1], spec_in[:, 0], precision=HIGH)
    image = field_of(jnp.stack([mix_re, mix_im], axis=1))

    def first_pass(index):
        start = index * block
        field = lifted_block(start)
        pre = spatial_block(image, start) + jnp.einsum('co,cak->oak', pw_float, field, precision=HIGH) + point_bias[:, None, None]
        incoming = lax.dynamic_slice_in_dim(cotangent, start, block, 1).astype(jnp.float32).reshape(channels, block * NY, NZ * NT)
        return (incoming * gelu_slope(pre)).astype(jnp.bfloat16)
    delta_blocks = lax.map(first_pass, block_ids)
    delta = lax.optimization_barrier(jnp.moveaxis(delta_blocks, 0, 1).reshape(channels, NX, NY, NZ * NT))

    def delta_block(start):
        return lax.dynamic_slice_in_dim(delta, start, block, 1).astype(jnp.float32).reshape(channels, block * NY, NZ * NT)
    spec_delta = spectra(delta_block)
    kappa = mode_weight[None, :, None, None]
    grad_re = kappa * (jnp.einsum('rmo,rmc->rmco', spec_delta[:, 0], spec_in[:, 0], precision=HIGH) + jnp.einsum('rmo,rmc->rmco', spec_delta[:, 1], spec_in[:, 1], precision=HIGH))
    grad_im = kappa * (jnp.einsum('rmo,rmc->rmco', spec_delta[:, 1], spec_in[:, 0], precision=HIGH) - jnp.einsum('rmo,rmc->rmco', spec_delta[:, 0], spec_in[:, 1], precision=HIGH))
    grad_spectral = jnp.stack([grad_re, grad_im]).reshape(2, modes_xy, modes_zt, channels * channels)
    back_re = jnp.einsum('rmco,rmo->rmc', weight[0], spec_delta[:, 0], precision=HIGH) + jnp.einsum('rmco,rmo->rmc', weight[1], spec_delta[:, 1], precision=HIGH)
    back_im = jnp.einsum('rmco,rmo->rmc', weight[0], spec_delta[:, 1], precision=HIGH) - jnp.einsum('rmco,rmo->rmc', weight[1], spec_delta[:, 0], precision=HIGH)
    back_image = field_of(jnp.stack([back_re, back_im], axis=1))

    def second_pass(index):
        start = index * block
        grad_field = spatial_block(back_image, start) + jnp.einsum('co,oak->cak', pw_float, delta_block(start), precision=HIGH)
        perm_piece = jnp.einsum('c,cazt->az', inject_gain[0], grad_field.reshape(channels, block * NY, NZ, NT), precision=HIGH)
        return (grad_field.astype(jnp.bfloat16), perm_piece.reshape(block, NY, NZ))
    grad_blocks, perm_blocks = lax.map(second_pass, block_ids)
    grad_input = jnp.moveaxis(grad_blocks, 0, 1).reshape(channels, NX, NY, NZ * NT)
    grad_perm = perm_blocks.reshape(NX, NY, NZ)
    return (grad_input, grad_spectral, grad_perm)
```

```python
import math

import jax
import jax.numpy as jnp
import ml_dtypes
import numpy as np
from jax import lax
from jax.experimental import pallas as pl
from jax.experimental.pallas import tpu as pltpu
from jax.sharding import PartitionSpec as P

C = 20
NX, NY, NZ, NT = 128, 128, 64, 16
MX, MY, MZ, MT = 24, 24, 24, 6
GX, GY = 16, 32
XL, YL = NX // GX, NY // GY
ML = MZ * MT // GX
RL = MX * MY // GY
ZT = NZ * NT
CY = C * YL
NMODE = 2 * MZ * MT
LANES = 768
RB = 384
BF = jnp.bfloat16
F32 = jnp.float32
MESH = pl.DeviceIdType.MESH
INV_ROOT_TWO = 1.0 / math.sqrt(2.0)
INV_ROOT_TWO_PI = 1.0 / math.sqrt(2.0 * math.pi)


def freq(j, n):
    return np.where(j < n // 2, j, j - n)


def lane_of(m, cy):
    if m < 6:
        return m * 128 + cy
    if cy < 48:
        return (m - 6) * 128 + 80 + cy
    return (m - 3) * 128 + 80 + cy - 48


def first_jx(d):
    return 3 * d // 4


def tables():
    jz, jt = np.divmod(np.arange(MZ * MT), MT)
    k = np.arange(ZT)
    turns = (freq(jz, MZ)[:, None] * (k // NT)[None] * NT + jt[:, None] * (k % NT)[None] * NZ) % ZT
    ang = 2 * np.pi / ZT * turns
    cos, sin = np.cos(ang) / math.sqrt(ZT), np.sin(ang) / math.sqrt(ZT)
    kap = np.where(jt == 0, 1.0, 2.0)[:, None]
    ft = np.stack([cos, -sin], 1).reshape(NMODE, ZT)
    inv = np.stack([kap * cos, -kap * sin], 1).reshape(NMODE, ZT)
    jx = np.arange(MX)
    ang = 2 * np.pi / NX * (freq(jx, MX)[:, None] * np.arange(NX)[None] % NX)
    cx = (np.cos(ang) / math.sqrt(NX)).reshape(MX, GX, XL)
    sx = (np.sin(ang) / math.sqrt(NX)).reshape(MX, GX, XL)
    wx = np.zeros((MX, 2, GX, 2, XL))
    wx[:, 0, :, 0], wx[:, 0, :, 1] = cx, sx
    wx[:, 1, :, 1], wx[:, 1, :, 0] = cx, -sx
    wx = wx.reshape(2 * MX, 2 * NX)
    xi = np.zeros((2 * NX, 128))
    xi[:, : 2 * MX] = wx.T
    perm = np.zeros((LANES, YL * 256))
    for m in range(ML):
        for c in range(C):
            for y in range(YL):
                perm[lane_of(m, c * YL + y), y * 256 + m * C + c] = 1
    pick = np.zeros((GY, YL, 2, 2, YL, MX, 2))
    for d in range(GY):
        for s in range(2):
            if s == 1 and d % 4 in (0, 3):
                continue
            for y in range(YL):
                for p in range(2):
                    pick[d, y, s, p, y, first_jx(d) + s, p] = 1
    pick = pick.reshape(GY * 16, YL * MX * 2)
    pick_pad = np.zeros((GY * 16, 256))
    pick_pad[:, : YL * MX * 2] = pick
    vc = np.zeros((GY, RL, 2, GY, YL, 2, 2))
    for d in range(GY):
        for i in range(RL):
            a, b = divmod(d * RL + i, MY)
            ang = 2 * np.pi / NY * (int(freq(np.array(b), MY)) * np.arange(NY) % NY)
            cy = (np.cos(ang) / math.sqrt(NY)).reshape(GY, YL)
            sy = (np.sin(ang) / math.sqrt(NY)).reshape(GY, YL)
            s = a - first_jx(d)
            vc[d, i, 0, :, :, s, 0], vc[d, i, 0, :, :, s, 1] = cy, sy
            vc[d, i, 1, :, :, s, 1], vc[d, i, 1, :, :, s, 0] = cy, -sy
    vc = vc.reshape(GY, 2 * RL, GY * 16)
    v_pad = np.zeros((GY, 48, GY * 16))
    v_pad[:, : 2 * RL] = vc
    u_pad = np.zeros((GY, GY * 16, 128))
    u_pad[:, :, : 2 * RL] = vc.transpose(0, 2, 1)
    rep = np.zeros((6, RB, 128))
    forms = [
        ((0, 1), (1, -1)),
        ((1, 1), (0, 1)),
        ((0, 1), (1, 1)),
        ((1, 1), (0, -1)),
        ((0, 1), (0, 1)),
        ((1, 1), (1, 1)),
    ]
    back = np.zeros((48, 2, RB))
    mask = np.zeros((RB, 256))
    kmask = np.zeros((2, RB, 256))
    for r in range(RL):
        for m in range(ML):
            for p in range(2):
                row = (r * ML + m) * 2 + p
                for f, form in enumerate(forms):
                    rep[f, row, 2 * r + form[p][0]] = form[p][1]
                back[2 * r, 0, row] = 1
                back[2 * r + 1, 1, row] = 1
                mask[row, m * C : (m + 1) * C] = 1
                for g in range(2):
                    kmask[g, row, m * C : (m + 1) * C] = 1 if (ML * g + m) % MT == 0 else 2
    spread = np.zeros((2, 256, 512))
    for m in range(ML):
        for c in range(C):
            for o in range(C):
                spread[0, m * C + c, c * C + o] = 1
                spread[1, m * C + o, c * C + o] = 1
    cell = np.zeros((XL, C, YL, XL, YL))
    for x in range(XL):
        for y in range(YL):
            cell[x, :, y, x, y] = 1
    cell = cell.reshape(XL * CY, XL * YL)
    chan = np.zeros((CY, C))
    chan[np.arange(CY), np.arange(CY) // YL] = 1
    chan_t = np.zeros((C, 128))
    chan_t[:, :CY] = chan.T
    same_y = np.zeros((CY, 128))
    same_y[:, :CY] = np.arange(CY)[:, None] % YL == np.arange(CY)[None] % YL
    ztrep = np.zeros((NZ + NT, ZT))
    ztrep[k // NT, k] = 1
    ztrep[NZ + k % NT, k] = 1
    zsum = np.zeros((ZT, 128))
    zsum[k, k // NT] = 1
    out = dict(
        ft=ft, inv=inv, wx=wx, xi=xi, perm=perm, perm_t=perm.T, pick=pick_pad, sel=pick.T,
        v=v_pad, u=u_pad, rep=rep.reshape(6 * RB, 128), back=back.reshape(48, 2 * RB),
        mask=mask, kmask=kmask, spread1=spread[0], spread2=spread[1],
        sum1=spread[1].T, sum2=spread[0].T, cell=cell, chan=chan, chan_t=chan_t,
        same_y=same_y, ztrep=ztrep, zsum=zsum,
    )
    return {n: np.ascontiguousarray(a).astype(ml_dtypes.bfloat16) for n, a in out.items()}


TABLE_ORDER = (
    "cell", "chan", "ztrep", "ft", "chan_t", "same_y", "wx", "perm", "pick", "v", "rep", "mask",
    "spread1", "sum1", "back", "u", "sel", "perm_t", "xi", "inv", "kmask", "spread2", "sum2", "zsum",
)
OWN = {"v": 32, "u": 32, "kmask": 2}


def dot(a, b):
    return lax.dot_general(a, b, (((1,), (0,)), ((), ())), preferred_element_type=F32)


def dot_nt(a, b):
    return lax.dot_general(a, b, (((1,), (1,)), ((), ())), preferred_element_type=F32)


def dot_tn(a, b):
    return lax.dot_general(a, b, (((0,), (0,)), ((), ())), preferred_element_type=F32)


def gelu_slope(v):
    a = jnp.abs(v) * INV_ROOT_TWO
    t = 1.0 / (1.0 + 0.3275911 * a)
    poly = t * (
        0.254829592
        + t * (-0.284496736 + t * (1.421413741 + t * (-1.453152027 + t * 1.061405429)))
    )
    e = jnp.exp(-0.5 * v * v)
    tail = 0.5 * poly * e
    return jnp.where(v >= 0, 1.0 - tail, tail) + v * e * INV_ROOT_TWO_PI


def split(a):
    hi = a.astype(BF)
    return hi, (a - hi.astype(F32)).astype(BF)


def kernel(*refs):
    names = TABLE_ORDER
    (x_hbm, cot_hbm, w_hbm, perm_ref, cells_ref, rates_ref, gain_ref, pw_ref, bias_ref) = refs[:9]
    hbm = dict(zip(names, refs[9 : 9 + len(names)]))
    pos = 9 + len(names)
    out_hbm, gs_hbm, gp_ref = refs[pos : pos + 3]
    pos += 3
    (
        x_v, cot_v, w_v, out_v, gs_v, lbf, base, cotf, wf, perm_s, stage, stage2, e00, e11,
        gxs, gxr, gys, gyr, gx_ss, gx_rs, gy_ss, gy_rs, in_sem, tab_sem, out_sem,
    ) = refs[pos : pos + 25]
    tab = dict(zip(names, refs[pos + 25 :]))
    gx = lax.axis_index("gx")
    gy = lax.axis_index("gy")

    def tab_copy(i):
        n = names[i]
        src = hbm[n]
        if n in OWN:
            src = src.at[lax.rem(gx, 2) if n == "kmask" else gy]
        return pltpu.make_async_copy(src, tab[n], tab_sem.at[i])

    waited = set()

    def need(*wanted):
        for n in wanted:
            if n not in waited:
                waited.add(n)
                tab_copy(names.index(n)).wait()
        got = tuple(tab[n][...] for n in wanted)
        return got if len(got) > 1 else got[0]

    x_in = pltpu.make_async_copy(x_hbm, x_v, in_sem.at[0])
    cot_in = pltpu.make_async_copy(cot_hbm, cot_v, in_sem.at[1])
    w_in = pltpu.make_async_copy(w_hbm, w_v, in_sem.at[2])
    x_in.start()
    for i in range(4):
        tab_copy(i).start()
    barrier = pltpu.get_barrier_semaphore()

    @pl.loop(1, GX)
    def _(o):
        pl.semaphore_signal(
            barrier, inc=1, device_id=(lax.rem(gx + o, GX), gy), device_id_type=MESH
        )

    @pl.loop(1, GY)
    def _(o):
        pl.semaphore_signal(
            barrier, inc=1, device_id=(gx, lax.rem(gy + o, GY)), device_id_type=MESH
        )

    cot_in.start()
    w_in.start()
    for i in range(4, len(names)):
        tab_copy(i).start()

    def gx_copy(step, o, landing):
        peer = lax.rem(gx + o, GX)
        return pltpu.make_async_remote_copy(
            src_ref=gxs.at[step, peer],
            dst_ref=gxr.at[step, landing],
            send_sem=gx_ss.at[step, o],
            recv_sem=gx_rs.at[step, o],
            device_id=(peer, gy),
            device_id_type=MESH,
        )

    def gy_copy(step, o, landing):
        peer = lax.rem(gy + o, GY)
        return pltpu.make_async_remote_copy(
            src_ref=gys.at[step, peer],
            dst_ref=gyr.at[step, landing],
            send_sem=gy_ss.at[step, o],
            recv_sem=gy_rs.at[step, o],
            device_id=(gx, peer),
            device_id_type=MESH,
        )

    def gx_wait(step):
        @pl.loop(1, GX)
        def _(o):
            gx_copy(step, o, lax.rem(gx + GX - o, GX)).wait_recv()

    def gy_wait(step):
        @pl.loop(1, GY)
        def _(o):
            gy_copy(step, o, lax.rem(gy + GY - o, GY)).wait_recv()

    def gy_send(step):
        @pl.loop(1, GY)
        def _(o):
            gy_copy(step, o, gy).start()

        gyr[step, gy] = gys[step, gy]

    lane = lax.broadcasted_iota(jnp.int32, (16, 128), 1)

    chan = need("chan")
    chan_f = chan.astype(F32)
    gain0 = jnp.sum(chan_f * gain_ref[0:1, :], axis=1, keepdims=True)
    gain1 = jnp.sum(chan_f * gain_ref[1:2, :], axis=1, keepdims=True)
    bias = jnp.sum(chan_f * bias_ref[...], axis=1, keepdims=True)

    for x in range(XL):
        perm_s[x * YL : (x + 1) * YL, :] = perm_ref[x]
    cell = need("cell")
    perm_hi, perm_lo = split(perm_s[...])
    col = lax.broadcasted_iota(jnp.int32, (XL * YL, 32), 0)
    cell_id = (gx * XL + col // YL) * NY + gy * YL + col % YL
    hits = (cells_ref[...] == cell_id).astype(BF)
    inflow = 0.5 * dot_nt(hits, rates_ref[...].astype(F32).astype(BF))
    perm_rows = dot(cell, perm_hi) + dot(cell, perm_lo)
    flow_rows = dot(cell, inflow.astype(BF))
    ztrep = need("ztrep")
    x_in.wait()
    ft = need("ft")

    def spread_rows(src, x, dst):
        for c in range(C):
            dst[c * YL : (c + 1) * YL, :] = src[c, x].astype(F32)

    for x in range(XL):
        rows = slice(x * CY, (x + 1) * CY)
        parts = jnp.concatenate([gain0 * perm_rows[rows], gain1 * flow_rows[rows]], axis=1)
        hi, lo = split(parts)
        added = dot(hi, ztrep) + dot(lo, ztrep)
        spread_rows(x_v, x, base.at[x])
        total = (base[x] + added).astype(BF)
        lbf[x, :CY] = total
        lbf[x, CY:] = total[:48]

    def zt_forward(field):
        for x in range(0, XL, 2):
            z = dot_nt(ft, field[x : x + 2].reshape(256, ZT))
            stage[:, x, :] = z[:, :128]
            stage[:, x + 1, :] = z[:, 128:]

    def pack(step, peer, into):
        blk = [
            stage[pl.ds((peer * ML + m) * 2, 2)].reshape(16, 128) for m in range(ML)
        ]
        for t in range(6):
            other = blk[6 + t] if t < 3 else pltpu.roll(blk[3 + t], 32, 1)
            into[:, t * 128 : (t + 1) * 128] = jnp.where(lane < 80, blk[t], other).astype(BF)

    def gx_send_packed(step):
        @pl.loop(1, GX)
        def _(o):
            peer = lax.rem(gx + o, GX)
            pack(step, peer, gxs.at[step, peer])
            gx_copy(step, o, gx).start()

        pack(step, gx, gxr.at[step, gx])

    def to_owners(step, gstep):
        got = gxr[step].reshape(256, LANES)
        xs = dot(need("wx"), got).astype(BF)
        ys = dot(xs, need("perm")).astype(BF)
        rows = jnp.concatenate(
            [ys[:, y * 256 : (y + 1) * 256] for y in range(YL)] + [jnp.zeros((64, 256), BF)], axis=0
        )
        gys[gstep] = dot(need("pick"), rows).astype(BF).reshape(GY, 16, 256)
        gy_send(gstep)

    def spectrum(gstep):
        spec = dot(need("v"), gyr[gstep].reshape(GY * 16, 256)).astype(BF)
        return jnp.concatenate([spec, jnp.zeros((80, 256), BF)], axis=0)

    def expand(spec, forms, mask, spread):
        rep = tab["rep"][forms * RB : (forms + 2) * RB, :]
        rows = dot(rep, spec).astype(BF) * jnp.concatenate([mask, mask], axis=0)
        return dot(rows, spread)

    def mixing(terms, summing, mask):
        wide = jnp.concatenate([wf[...], wf[...]], axis=0)
        rows = dot((terms * wide).astype(BF), summing).astype(BF)
        rows = rows * jnp.concatenate([mask, mask], axis=0)
        mixed = dot(need("back"), rows).astype(BF)
        return jnp.concatenate([mixed, jnp.zeros((80, 256), BF)], axis=0)

    def spread_y(gstep, mixed):
        gys[gstep] = dot(need("u"), mixed).astype(BF).reshape(GY, 16, 256)
        gy_send(gstep)

    def to_columns(gstep, step):
        ys = dot(need("sel"), gyr[gstep].reshape(GY * 16, 256)).astype(BF)
        wide = jnp.concatenate([ys[y * 48 : (y + 1) * 48] for y in range(YL)], axis=1)
        xs = dot(wide, need("perm_t")).astype(BF)
        xs = jnp.concatenate([xs, jnp.zeros((80, LANES), BF)], axis=0)
        gxs[step] = dot(need("xi"), xs).astype(BF).reshape(GX, 16, LANES)

        @pl.loop(1, GX)
        def _(o):
            gx_copy(step, o, gx).start()

        gxr[step, gx] = gxs[step, gx]

    def unpack(step, src):
        got = [gxr[step, src, :, t * 128 : (t + 1) * 128].astype(F32) for t in range(6)]
        for m in range(ML):
            if m < 6:
                v = got[m]
            else:
                v = jnp.where(
                    lane < 48, pltpu.roll(got[m - 6], 48, 1), pltpu.roll(got[m - 3], 96, 1)
                )
            stage2[pl.ds((src * ML + m) * 2, 2)] = v.reshape(2, 8, 128)

    def receive_images(step):
        unpack(step, gx)

        @pl.loop(1, GX)
        def _(o):
            src = lax.rem(gx + GX - o, GX)
            gx_copy(step, o, src).wait_recv()
            unpack(step, src)

    zt_forward(lbf)
    pl.semaphore_wait(barrier, GX + GY - 2)
    gx_send_packed(0)

    chan_t, same_y = need("chan_t", "same_y")
    pw = pw_ref[...]
    pw_fwd = (dot(dot_nt(chan, pw).astype(BF), chan_t) * same_y.astype(F32)).astype(BF)
    pw_bwd = (dot(dot(chan, pw).astype(BF), chan_t) * same_y.astype(F32)).astype(BF)
    for x in range(XL):
        base[x] = dot(pw_fwd, lbf[x]) + bias
    w_in.wait()
    wf[...] = jnp.zeros((RB, 512), F32)
    for i in range(RL * ML):
        wf[2 * i : 2 * i + 2, :400] = w_v[i].astype(F32)

    gx_wait(0)
    to_owners(0, 0)
    cot_in.wait()
    for x in range(XL):
        spread_rows(cot_v, x, cotf.at[x])
    need("rep")
    mask, spread1, sum1 = need("mask", "spread1", "sum1")
    gy_wait(0)
    spec_in = spectrum(0)
    spread_y(1, mixing(expand(spec_in, 0, mask, spread1), sum1, mask))
    kmask = need("kmask")
    both = expand(spec_in, 4, kmask, spread1)
    e00[...] = both[:RB]
    e11[...] = both[RB:]
    gy_wait(1)
    to_columns(1, 1)
    inv = need("inv")
    receive_images(1)
    for x in range(XL):
        image = dot_tn(stage2[:, x, :].astype(BF), inv)
        pre = base[x] + image[:CY]
        delta = (cotf[x] * gelu_slope(pre)).astype(BF)
        lbf[x, :CY] = delta
        lbf[x, CY:] = delta[:48]

    zt_forward(lbf)
    gx_send_packed(2)
    for x in range(XL):
        base[x] = dot(pw_bwd, lbf[x])
    spread2, sum2 = need("spread2", "sum2")
    gx_wait(2)
    to_owners(2, 2)
    gy_wait(2)
    terms = expand(spectrum(2), 2, mask, spread2)
    spread_y(3, mixing(terms, sum2, mask))
    grad = terms[:RB] * e00[...] + terms[RB:] * e11[...]
    wf[...] = grad
    for i in range(RL * ML):
        gs_v[i] = wf[2 * i : 2 * i + 2, :400]
    gs_out = pltpu.make_async_copy(gs_v, gs_hbm, out_sem.at[XL])
    gs_out.start()
    gy_wait(3)
    to_columns(3, 3)
    zsum = need("zsum")
    receive_images(3)

    def out_copy(x):
        return pltpu.make_async_copy(out_v.at[:, x], out_hbm.at[:, x], out_sem.at[x])

    for x in range(XL):
        image = dot_tn(stage2[:, x, :].astype(BF), inv)
        field = base[x] + image[:CY]
        cotf[x] = field
        for c in range(C):
            out_v[c, x] = cotf[x, c * YL : (c + 1) * YL, :].astype(BF)
        out_copy(x).start()
        hi, lo = split(field * gain0)
        zs = dot(hi, zsum) + dot(lo, zsum)
        acc = zs[:8]
        for c in range(1, CY // 8):
            acc = acc + zs[8 * c : 8 * c + 8]
        gp_ref[x] = (acc[:4] + acc[4:])[:, :NZ]

    for x in range(XL):
        out_copy(x).wait()
    gs_out.wait()
    for step in range(4):

        @pl.loop(1, GX)
        def _(o):
            gx_copy(step, o, gx).wait_send()

        @pl.loop(1, GY)
        def _(o):
            gy_copy(step, o, gy).wait_send()


def on_device(
    layer_input, cotangent, log_perm, well_cells, well_rates, inject_gain, spectral_weight,
    point_weight, point_bias,
):
    table = tables()
    weight = jnp.transpose(spectral_weight, (1, 2, 0, 3)).reshape(RL * ML, 2, C * C)
    hbm = pl.BlockSpec(memory_space=pl.ANY)
    vmem = pl.BlockSpec(memory_space=pltpu.VMEM)
    scratch = [
        pltpu.VMEM((C, XL, YL, ZT), BF),
        pltpu.VMEM((C, XL, YL, ZT), BF),
        pltpu.VMEM((RL * ML, 2, C * C), BF),
        pltpu.VMEM((C, XL, YL, ZT), BF),
        pltpu.VMEM((RL * ML, 2, C * C), F32),
        pltpu.VMEM((XL, 128, ZT), BF),
        pltpu.VMEM((XL, CY, ZT), F32),
        pltpu.VMEM((XL, CY, ZT), F32),
        pltpu.VMEM((RB, 512), F32),
        pltpu.VMEM((XL * YL, NZ), F32),
        pltpu.VMEM((NMODE, XL, 128), F32),
        pltpu.VMEM((NMODE, XL, 128), F32),
        pltpu.VMEM((RB, 512), F32),
        pltpu.VMEM((RB, 512), F32),
        pltpu.VMEM((4, GX, 16, LANES), BF),
        pltpu.VMEM((4, GX, 16, LANES), BF),
        pltpu.VMEM((4, GY, 16, 256), BF),
        pltpu.VMEM((4, GY, 16, 256), BF),
        pltpu.SemaphoreType.DMA((4, GX)),
        pltpu.SemaphoreType.DMA((4, GX)),
        pltpu.SemaphoreType.DMA((4, GY)),
        pltpu.SemaphoreType.DMA((4, GY)),
        pltpu.SemaphoreType.DMA((3,)),
        pltpu.SemaphoreType.DMA((len(TABLE_ORDER),)),
        pltpu.SemaphoreType.DMA((XL + 1,)),
    ]
    for n in TABLE_ORDER:
        shape = table[n].shape[1:] if n in OWN else table[n].shape
        scratch.append(pltpu.VMEM(shape, BF))
    grad_input, grad_spec, grad_perm = pl.pallas_call(
        kernel,
        out_shape=(
            jax.ShapeDtypeStruct((C, XL, YL, ZT), BF),
            jax.ShapeDtypeStruct((RL * ML, 2, C * C), F32),
            jax.ShapeDtypeStruct((XL, YL, NZ), F32),
        ),
        in_specs=[hbm] * 3 + [vmem] * 6 + [hbm] * len(TABLE_ORDER),
        out_specs=(hbm, hbm, vmem),
        scratch_shapes=scratch,
        compiler_params=pltpu.CompilerParams(
            collective_id=0, has_side_effects=True, vmem_limit_bytes=56 * 1024 * 1024
        ),
    )(
        layer_input, cotangent, weight, log_perm, well_cells.reshape(1, -1), well_rates.T,
        inject_gain, point_weight, point_bias.reshape(1, -1),
        *[jnp.asarray(table[n]) for n in TABLE_ORDER],
    )
    grad_spec = jnp.transpose(grad_spec.reshape(RL, ML, 2, C * C), (2, 0, 1, 3))
    return grad_input, grad_spec, grad_perm


def solution(mesh):
    return jax.shard_map(
        on_device,
        mesh=mesh,
        in_specs=(
            P(None, "gx", "gy", None),
            P(None, "gx", "gy", None),
            P("gx", "gy", None),
            P(),
            P(),
            P(),
            P(None, "gy", "gx", None),
            P(),
            P(),
        ),
        out_specs=(P(None, "gx", "gy", None), P(None, "gy", "gx", None), P("gx", "gy", None)),
        check_vma=False,
    )
```

```python
import math

import jax
import jax.numpy as jnp
import ml_dtypes
import numpy as np
from jax import lax
from jax.experimental import pallas as pl
from jax.experimental.pallas import tpu as pltpu
from jax.sharding import PartitionSpec as P

C = 20
NX, NY, NZ, NT = 128, 128, 64, 16
MX, MY, MZ, MT = 24, 24, 24, 6
GX, GY = 16, 32
XL, YL = NX // GX, NY // GY
ML = MZ * MT // GX
RL = MX * MY // GY
ZT = NZ * NT
CY = C * YL
NMODE = 2 * MZ * MT
NQ = 3
MQ = ML // NQ
LANES = 256
QL = 128
RB = 128
BF = jnp.bfloat16
F32 = jnp.float32
MESH = pl.DeviceIdType.MESH
INV_ROOT_TWO = 1.0 / math.sqrt(2.0)
INV_ROOT_TWO_PI = 1.0 / math.sqrt(2.0 * math.pi)


def freq(j, n):
    return np.where(j < n // 2, j, j - n)


def lane_of(m, cy):
    if m == 0:
        return cy
    if m == 2:
        return 128 + cy
    return 80 + cy if cy < 48 else 208 + cy - 48


X_FAR = [8] + [o for k in range(7, 0, -1) for o in (k, GX - k)]
Y_FAR = sorted(
    ((dz, dx) for dz in range(8) for dx in range(4) if dz or dx),
    key=lambda d: -(min(d[0], 8 - d[0]) + min(d[1], 4 - d[1])),
)


def first_jx(d):
    return 3 * d // 4


def tables():
    jz, jt = np.divmod(np.arange(MZ * MT), MT)
    k = np.arange(ZT)
    turns = (freq(jz, MZ)[:, None] * (k // NT)[None] * NT + jt[:, None] * (k % NT)[None] * NZ) % ZT
    ang = 2 * np.pi / ZT * turns
    cos, sin = np.cos(ang) / math.sqrt(ZT), np.sin(ang) / math.sqrt(ZT)
    kap = np.where(jt == 0, 1.0, 2.0)[:, None]
    ft = np.stack([cos, -sin], 1)
    inv = np.stack([kap * cos, -kap * sin], 1)

    def by_chunk(a):
        return a.reshape(GX, NQ, MQ, 2, ZT).transpose(1, 0, 2, 3, 4).reshape(NMODE, ZT)

    ft, inv = by_chunk(ft), by_chunk(inv)
    jx = np.arange(MX)
    ang = 2 * np.pi / NX * (freq(jx, MX)[:, None] * np.arange(NX)[None] % NX)
    cx = (np.cos(ang) / math.sqrt(NX)).reshape(MX, GX, XL)
    sx = (np.sin(ang) / math.sqrt(NX)).reshape(MX, GX, XL)
    wx = np.zeros((MX, 2, GX, 2, XL))
    wx[:, 0, :, 0], wx[:, 0, :, 1] = cx, sx
    wx[:, 1, :, 1], wx[:, 1, :, 0] = cx, -sx
    wx = wx.reshape(2 * MX, 2 * NX)
    xi = np.zeros((2 * NX, 128))
    xi[:, : 2 * MX] = wx.T
    perm = np.zeros((LANES, YL * QL))
    for m in range(MQ):
        for c in range(C):
            for y in range(YL):
                perm[lane_of(m, c * YL + y), y * QL + m * C + c] = 1
    pick = np.zeros((GY, YL, 2, 2, YL, MX, 2))
    for d in range(GY):
        for s in range(2):
            if s == 1 and d % 4 in (0, 3):
                continue
            for y in range(YL):
                for p in range(2):
                    pick[d, y, s, p, y, first_jx(d) + s, p] = 1
    pick = pick.reshape(GY * 16, YL * MX * 2)
    pick_pad = np.zeros((GY * 16, 256))
    pick_pad[:, : YL * MX * 2] = pick
    vc = np.zeros((GY, RL, 2, GY, YL, 2, 2))
    for d in range(GY):
        for i in range(RL):
            a, b = divmod(d * RL + i, MY)
            ang = 2 * np.pi / NY * (int(freq(np.array(b), MY)) * np.arange(NY) % NY)
            cy = (np.cos(ang) / math.sqrt(NY)).reshape(GY, YL)
            sy = (np.sin(ang) / math.sqrt(NY)).reshape(GY, YL)
            s = a - first_jx(d)
            vc[d, i, 0, :, :, s, 0], vc[d, i, 0, :, :, s, 1] = cy, sy
            vc[d, i, 1, :, :, s, 1], vc[d, i, 1, :, :, s, 0] = cy, -sy
    vc = vc.reshape(GY, 2 * RL, GY * 16)
    v_pad = np.zeros((GY, 48, GY * 16))
    v_pad[:, : 2 * RL] = vc
    u_pad = np.zeros((GY, GY * 16, 128))
    u_pad[:, :, : 2 * RL] = vc.transpose(0, 2, 1)
    rep = np.zeros((6, RB, 128))
    forms = [
        ((0, 1), (1, -1)),
        ((1, 1), (0, 1)),
        ((0, 1), (1, 1)),
        ((1, 1), (0, -1)),
        ((0, 1), (0, 1)),
        ((1, 1), (1, 1)),
    ]
    back = np.zeros((48, 2, RB))
    mask = np.zeros((RB, QL))
    kmask = np.zeros((2, RB, QL))
    for r in range(RL):
        for m in range(MQ):
            for p in range(2):
                row = (r * MQ + m) * 2 + p
                for f, form in enumerate(forms):
                    rep[f, row, 2 * r + form[p][0]] = form[p][1]
                back[2 * r, 0, row] = 1
                back[2 * r + 1, 1, row] = 1
                mask[row, m * C : (m + 1) * C] = 1
                for g in range(2):
                    kmask[g, row, m * C : (m + 1) * C] = 1 if (MQ * g + m) % MT == 0 else 2
    spread = np.zeros((2, QL, 512))
    for m in range(MQ):
        for c in range(C):
            for o in range(C):
                spread[0, m * C + c, c * C + o] = 1
                spread[1, m * C + o, c * C + o] = 1
    cell = np.zeros((XL, C, YL, XL, YL))
    for x in range(XL):
        for y in range(YL):
            cell[x, :, y, x, y] = 1
    cell = cell.reshape(XL * CY, XL * YL)
    chan = np.zeros((CY, C))
    chan[np.arange(CY), np.arange(CY) // YL] = 1
    chan_t = np.zeros((C, 128))
    chan_t[:, :CY] = chan.T
    same_y = np.zeros((CY, 128))
    same_y[:, :CY] = np.arange(CY)[:, None] % YL == np.arange(CY)[None] % YL
    ztrep = np.zeros((NZ + NT, ZT))
    ztrep[k // NT, k] = 1
    ztrep[NZ + k % NT, k] = 1
    zsum = np.zeros((ZT, 128))
    zsum[k, k // NT] = 1
    out = dict(
        ft=ft, inv=inv, wx=wx, xi=xi, perm=perm, perm_t=perm.T, pick=pick_pad, sel=pick.T,
        v=v_pad, u=u_pad, rep=rep.reshape(6 * RB, 128), back=back.reshape(48, 2 * RB),
        mask=mask, kmask=kmask, spread1=spread[0], spread2=spread[1],
        sum1=spread[1].T, sum2=spread[0].T, cell=cell, chan=chan, chan_t=chan_t,
        same_y=same_y, ztrep=ztrep, zsum=zsum,
    )
    return {n: np.ascontiguousarray(a).astype(ml_dtypes.bfloat16) for n, a in out.items()}


TABLE_ORDER = (
    "cell", "chan", "ztrep", "ft", "chan_t", "same_y", "wx", "perm", "pick", "v", "rep", "mask",
    "spread1", "sum1", "back", "u", "sel", "perm_t", "xi", "inv", "kmask", "spread2", "sum2", "zsum",
)
OWN = ("v", "u")


def dot(a, b):
    return lax.dot_general(a, b, (((1,), (0,)), ((), ())), preferred_element_type=F32)


def dot_nt(a, b):
    return lax.dot_general(a, b, (((1,), (1,)), ((), ())), preferred_element_type=F32)


def dot_tn(a, b):
    return lax.dot_general(a, b, (((0,), (0,)), ((), ())), preferred_element_type=F32)


def gelu_slope(v):
    a = jnp.abs(v) * INV_ROOT_TWO
    t = 1.0 / (1.0 + 0.3275911 * a)
    poly = t * (
        0.254829592
        + t * (-0.284496736 + t * (1.421413741 + t * (-1.453152027 + t * 1.061405429)))
    )
    e = jnp.exp(-0.5 * v * v)
    tail = 0.5 * poly * e
    return jnp.where(v >= 0, 1.0 - tail, tail) + v * e * INV_ROOT_TWO_PI


def split(a):
    hi = a.astype(BF)
    return hi, (a - hi.astype(F32)).astype(BF)


def kernel(*refs):
    names = TABLE_ORDER
    (x_hbm, cot_hbm, w_hbm, perm_ref, cells_ref, rates_ref, gain_ref, pw_ref, bias_ref) = refs[:9]
    hbm = dict(zip(names, refs[9 : 9 + len(names)]))
    pos = 9 + len(names)
    out_hbm, gs_hbm, gp_ref = refs[pos : pos + 3]
    pos += 3
    (
        x_v, cot_v, w_v, out_v, gs_v, lbf, base, cotf, wf, perm_s, stage, stage2, e00, e11, grad, spec_in,
        gxs, gxr, gys, gyr, gx_ss, gx_rs, gy_ss, gy_rs, in_sem, tab_sem, out_sem,
    ) = refs[pos : pos + 27]
    tab = dict(zip(names, refs[pos + 27 :]))
    gx = lax.axis_index("gx")
    gy = lax.axis_index("gy")

    def tab_copy(i):
        n = names[i]
        src = hbm[n]
        if n in OWN:
            src = src.at[gy]
        return pltpu.make_async_copy(src, tab[n], tab_sem.at[i])

    waited = set()

    def need(*wanted):
        for n in wanted:
            if n not in waited:
                waited.add(n)
                tab_copy(names.index(n)).wait()
        got = tuple(tab[n][...] for n in wanted)
        return got if len(got) > 1 else got[0]

    x_in = pltpu.make_async_copy(x_hbm, x_v, in_sem.at[0])
    cot_in = pltpu.make_async_copy(cot_hbm, cot_v, in_sem.at[1])
    w_in = pltpu.make_async_copy(w_hbm, w_v, in_sem.at[2])
    x_in.start()
    for i in range(4):
        tab_copy(i).start()
    barrier = pltpu.get_barrier_semaphore()

    @pl.loop(1, GX)
    def _(o):
        pl.semaphore_signal(
            barrier, inc=1, device_id=(lax.rem(gx + o, GX), gy), device_id_type=MESH
        )

    @pl.loop(1, GY)
    def _(o):
        pl.semaphore_signal(
            barrier, inc=1, device_id=(gx, lax.rem(gy + o, GY)), device_id_type=MESH
        )

    def gx_copy(step, q, o, landing):
        peer = lax.rem(gx + o, GX)
        return pltpu.make_async_remote_copy(
            src_ref=gxs.at[step * NQ + q, peer],
            dst_ref=gxr.at[step * NQ + q, landing],
            send_sem=gx_ss.at[step * NQ + q],
            recv_sem=gx_rs.at[step * NQ + q],
            device_id=(peer, gy),
            device_id_type=MESH,
        )

    def gy_copy(step, q, o, landing):
        peer = lax.rem(gy // 4 + o[0], 8) * 4 + lax.rem(gy + o[1], 4)
        return pltpu.make_async_remote_copy(
            src_ref=gys.at[step * NQ + q, peer],
            dst_ref=gyr.at[step * NQ + q, landing],
            send_sem=gy_ss.at[step * NQ + q],
            recv_sem=gy_rs.at[step * NQ + q],
            device_id=(gx, peer),
            device_id_type=MESH,
        )

    def all_blocks(buf, sem, i, peers):
        blocks = buf.at[i, pl.ds(0, peers - 1)]
        return pltpu.make_async_copy(blocks, blocks, sem.at[i])

    def gx_wait(step, q):
        all_blocks(gxr, gx_rs, step * NQ + q, GX).wait()

    def gy_wait(step, q):
        all_blocks(gyr, gy_rs, step * NQ + q, GY).wait()

    def gy_send(step, q):
        for o in Y_FAR:
            gy_copy(step, q, o, gy).start()
        gyr[step * NQ + q, gy] = gys[step * NQ + q, gy]

    lane = lax.broadcasted_iota(jnp.int32, (16, 128), 1)

    chan = need("chan")
    chan_f = chan.astype(F32)
    gain0 = jnp.sum(chan_f * gain_ref[0:1, :], axis=1, keepdims=True)
    gain1 = jnp.sum(chan_f * gain_ref[1:2, :], axis=1, keepdims=True)
    bias = jnp.sum(chan_f * bias_ref[...], axis=1, keepdims=True)

    for x in range(XL):
        perm_s[x * YL : (x + 1) * YL, :] = perm_ref[x]
    cell = need("cell")
    perm_hi, perm_lo = split(perm_s[...])
    col = lax.broadcasted_iota(jnp.int32, (XL * YL, 32), 0)
    cell_id = (gx * XL + col // YL) * NY + gy * YL + col % YL
    hits = (cells_ref[...] == cell_id).astype(BF)
    inflow = 0.5 * dot_nt(hits, rates_ref[...].astype(F32).astype(BF))
    perm_rows = dot(cell, perm_hi) + dot(cell, perm_lo)
    flow_rows = dot(cell, inflow.astype(BF))
    ztrep = need("ztrep")
    ft = need("ft")
    x_in.wait()
    w_in.start()
    for i in range(4, 10):
        tab_copy(i).start()
    cot_in.start()
    for i in range(10, len(names)):
        tab_copy(i).start()

    def spread_rows(src, x, dst):
        for c in range(C):
            dst[c * YL : (c + 1) * YL, :] = src[c, x].astype(F32)

    for x in range(XL):
        rows = slice(x * CY, (x + 1) * CY)
        parts = jnp.concatenate([gain0 * perm_rows[rows], gain1 * flow_rows[rows]], axis=1)
        hi, lo = split(parts)
        added = dot(hi, ztrep) + dot(lo, ztrep)
        spread_rows(x_v, x, base.at[x])
        total = (base[x] + added).astype(BF)
        lbf[x, :CY] = total
        lbf[x, CY:] = total[:48]

    def zt_forward(field):
        for x in range(0, XL, 2):
            z = dot_nt(ft, field[x : x + 2].reshape(256, ZT))
            stage[:, x, :] = z[:, :128]
            stage[:, x + 1, :] = z[:, 128:]

    def pack(q, peer, into):
        row = (q * GX + peer) * MQ * 2
        blk = [stage[pl.ds(row + 2 * m, 2)].reshape(16, 128) for m in range(MQ)]
        into[:, :128] = jnp.where(lane < 80, blk[0], blk[1]).astype(BF)
        into[:, 128:] = jnp.where(lane < 80, blk[2], pltpu.roll(blk[1], 32, 1)).astype(BF)

    def gx_send(step, q):
        for o in X_FAR:
            gx_copy(step, q, o, gx).start()
        gxr[step * NQ + q, gx] = gxs[step * NQ + q, gx]

    def gx_send_packed(step):
        for q in range(NQ):
            for peer in range(GX):
                pack(q, peer, gxs.at[step * NQ + q, peer])
            gx_send(step, q)

    def to_owners(step, q):
        gx_wait(step, q)
        got = gxr[step * NQ + q].reshape(256, LANES)
        xs = dot(need("wx"), got).astype(BF)
        ys = dot(xs, need("perm")).astype(BF)
        rows = jnp.concatenate(
            [ys[:, y * QL : (y + 1) * QL] for y in range(YL)] + [jnp.zeros((64, QL), BF)], axis=0
        )
        gys[step * NQ + q] = dot(need("pick"), rows).astype(BF).reshape(GY, 16, QL)
        gy_send(step, q)

    def spectrum(step, q):
        gy_wait(step, q)
        spec = dot(need("v"), gyr[step * NQ + q].reshape(GY * 16, QL)).astype(BF)
        return jnp.concatenate([spec, jnp.zeros((80, QL), BF)], axis=0)

    def expand(spec, forms, mask, spread):
        rep = tab["rep"][forms * RB : (forms + 2) * RB, :]
        rows = dot(rep, spec).astype(BF) * jnp.concatenate([mask, mask], axis=0)
        return dot(rows, spread)

    def mix(step, q, terms, summing):
        mask = need("mask")
        wide = jnp.concatenate([wf[q], wf[q]], axis=0)
        rows = dot((terms * wide).astype(BF), summing).astype(BF)
        rows = rows * jnp.concatenate([mask, mask], axis=0)
        mixed = dot(need("back"), rows).astype(BF)
        mixed = jnp.concatenate([mixed, jnp.zeros((80, QL), BF)], axis=0)
        gys[step * NQ + q] = dot(need("u"), mixed).astype(BF).reshape(GY, 16, QL)
        gy_send(step, q)

    def to_columns(step, q):
        gy_wait(step, q)
        ys = dot(need("sel"), gyr[step * NQ + q].reshape(GY * 16, QL)).astype(BF)
        wide = jnp.concatenate([ys[y * 48 : (y + 1) * 48] for y in range(YL)], axis=1)
        xs = dot(wide, need("perm_t")).astype(BF)
        xs = jnp.concatenate([xs, jnp.zeros((80, LANES), BF)], axis=0)
        gxs[step * NQ + q] = dot(need("xi"), xs).astype(BF).reshape(GX, 16, LANES)
        gx_send(step, q)

    def unpack(step, q, src):
        got = [
            gxr[step * NQ + q, src, :, t * 128 : (t + 1) * 128].astype(F32) for t in range(2)
        ]
        middle = jnp.where(lane < 48, pltpu.roll(got[0], 48, 1), pltpu.roll(got[1], 96, 1))
        row = (q * GX + src) * MQ * 2
        for m, v in enumerate((got[0], middle, got[1])):
            stage2[row + 2 * m : row + 2 * m + 2] = v.reshape(2, 8, 128)

    def receive_images(step, q):
        gx_wait(step, q)
        for src in range(GX):
            unpack(step, q, src)

    def exchange(step, middle, beside):
        beside(0)
        for q in range(NQ):
            to_owners(step, q)
        beside(1)
        for q in range(NQ):
            middle(q)
        beside(2)
        for q in range(NQ):
            to_columns(step + 1, q)
        beside(3)
        for q in range(NQ):
            receive_images(step + 1, q)

    zt_forward(lbf)
    pl.semaphore_wait(barrier, GX + GY - 2)
    gx_send_packed(0)

    chan_t, same_y = need("chan_t", "same_y")
    pw = pw_ref[...]
    pw_fwd = (dot(dot_nt(chan, pw).astype(BF), chan_t) * same_y.astype(F32)).astype(BF)
    pw_bwd = (dot(dot(chan, pw).astype(BF), chan_t) * same_y.astype(F32)).astype(BF)

    def forward_middle(q):
        spec = spectrum(0, q)
        spec_in[q] = spec
        mix(1, q, expand(spec, 0, need("mask"), need("spread1")), need("sum1"))

    def forward_beside(slot):
        if slot == 0:
            need("rep")
            w_in.wait()
            wf[...] = jnp.zeros((NQ, RB, 512), F32)
            for r in range(RL):
                for m in range(ML):
                    q, row = m // MQ, (r * MQ + m % MQ) * 2
                    wf[q, row : row + 2, :400] = w_v[r * ML + m].astype(F32)
            for x in range(XL):
                base[x] = dot(pw_fwd, lbf[x]) + bias
            cot_in.wait()
            for x in range(XL):
                spread_rows(cot_v, x, cotf.at[x])
        if slot == 3:
            need("kmask")
            for q in range(NQ):
                kmask = tab["kmask"][lax.rem(gx + q, 2)]
                both = expand(spec_in[q], 4, kmask, need("spread1"))
                e00[q] = both[:RB]
                e11[q] = both[RB:]

    exchange(0, forward_middle, forward_beside)
    inv = need("inv")
    for x in range(XL):
        image = dot_tn(stage2[:, x, :].astype(BF), inv)
        pre = base[x] + image[:CY]
        delta = (cotf[x] * gelu_slope(pre)).astype(BF)
        lbf[x, :CY] = delta
        lbf[x, CY:] = delta[:48]

    zt_forward(lbf)
    gx_send_packed(2)
    gs_out = pltpu.make_async_copy(gs_v, gs_hbm, out_sem.at[XL])

    def backward_middle(q):
        terms = expand(spectrum(2, q), 2, need("mask"), need("spread2"))
        mix(3, q, terms, need("sum2"))
        grad[q] = terms[:RB] * e00[q] + terms[RB:] * e11[q]

    def backward_beside(slot):
        if slot == 0:
            for x in range(XL):
                base[x] = dot(pw_bwd, lbf[x])
        if slot == 3:
            for r in range(RL):
                for m in range(ML):
                    q, row = m // MQ, (r * MQ + m % MQ) * 2
                    gs_v[r * ML + m] = grad[q, row : row + 2, :400]
            gs_out.start()

    exchange(2, backward_middle, backward_beside)
    zsum = need("zsum")

    def out_copy(x):
        return pltpu.make_async_copy(out_v.at[:, x], out_hbm.at[:, x], out_sem.at[x])

    for x in range(XL):
        image = dot_tn(stage2[:, x, :].astype(BF), inv)
        field = base[x] + image[:CY]
        cotf[x] = field
        for c in range(C):
            out_v[c, x] = cotf[x, c * YL : (c + 1) * YL, :].astype(BF)
        out_copy(x).start()
        hi, lo = split(field * gain0)
        zs = dot(hi, zsum) + dot(lo, zsum)
        acc = zs[:8]
        for c in range(1, CY // 8):
            acc = acc + zs[8 * c : 8 * c + 8]
        gp_ref[x] = (acc[:4] + acc[4:])[:, :NZ]

    for x in range(XL):
        out_copy(x).wait()
    gs_out.wait()
    for i in range(4 * NQ):
        all_blocks(gxs, gx_ss, i, GX).wait()
        all_blocks(gys, gy_ss, i, GY).wait()


def hand_over(*refs):
    given, result, held, (in_sem, out_sem) = refs[:3], refs[3:6], refs[6:9], refs[9:]
    part = C // 5
    places = [(0, pl.ds(i * part, part)) for i in range(5)] + [(1, slice(None)), (2, slice(None))]
    ins, outs = [], []
    for i, (a, at) in enumerate(places):
        ins.append(pltpu.make_async_copy(given[a].at[at], held[a].at[at], in_sem.at[i]))
        outs.append(pltpu.make_async_copy(held[a].at[at], result[a].at[at], out_sem.at[i]))
    for c in ins:
        c.start()
    for a, b in zip(ins, outs):
        a.wait()
        b.start()
    for c in outs:
        c.wait()


def on_device(
    layer_input, cotangent, log_perm, well_cells, well_rates, inject_gain, spectral_weight,
    point_weight, point_bias,
):
    table = tables()
    weight = jnp.transpose(spectral_weight, (1, 2, 0, 3)).reshape(RL * ML, 2, C * C)
    hbm = pl.BlockSpec(memory_space=pl.ANY)
    vmem = pl.BlockSpec(memory_space=pltpu.VMEM)
    scratch = [
        pltpu.VMEM((C, XL, YL, ZT), BF),
        pltpu.VMEM((C, XL, YL, ZT), BF),
        pltpu.VMEM((RL * ML, 2, C * C), BF),
        pltpu.VMEM((C, XL, YL, ZT), BF),
        pltpu.VMEM((RL * ML, 2, C * C), F32),
        pltpu.VMEM((XL, 128, ZT), BF),
        pltpu.VMEM((XL, CY, ZT), F32),
        pltpu.VMEM((XL, CY, ZT), F32),
        pltpu.VMEM((NQ, RB, 512), F32),
        pltpu.VMEM((XL * YL, NZ), F32),
        pltpu.VMEM((NMODE, XL, 128), F32),
        pltpu.VMEM((NMODE, XL, 128), F32),
        pltpu.VMEM((NQ, RB, 512), F32),
        pltpu.VMEM((NQ, RB, 512), F32),
        pltpu.VMEM((NQ, RB, 512), F32),
        pltpu.VMEM((NQ, QL, QL), BF),
        pltpu.VMEM((4 * NQ, GX, 16, LANES), BF),
        pltpu.VMEM((4 * NQ, GX, 16, LANES), BF),
        pltpu.VMEM((4 * NQ, GY, 16, QL), BF),
        pltpu.VMEM((4 * NQ, GY, 16, QL), BF),
        pltpu.SemaphoreType.DMA((4 * NQ,)),
        pltpu.SemaphoreType.DMA((4 * NQ,)),
        pltpu.SemaphoreType.DMA((4 * NQ,)),
        pltpu.SemaphoreType.DMA((4 * NQ,)),
        pltpu.SemaphoreType.DMA((3,)),
        pltpu.SemaphoreType.DMA((len(TABLE_ORDER),)),
        pltpu.SemaphoreType.DMA((XL + 1,)),
    ]
    for n in TABLE_ORDER:
        shape = table[n].shape[1:] if n in OWN else table[n].shape
        scratch.append(pltpu.VMEM(shape, BF))
    results = (
        jax.ShapeDtypeStruct((C, XL, YL, ZT), BF),
        jax.ShapeDtypeStruct((RL * ML, 2, C * C), F32),
        jax.ShapeDtypeStruct((XL, YL, NZ), F32),
    )
    done = pl.pallas_call(
        kernel,
        out_shape=results,
        in_specs=[hbm] * 3 + [vmem] * 6 + [hbm] * len(TABLE_ORDER),
        out_specs=(hbm, hbm, vmem),
        scratch_shapes=scratch,
        compiler_params=pltpu.CompilerParams(
            collective_id=0, has_side_effects=True, vmem_limit_bytes=56 * 1024 * 1024
        ),
    )(
        layer_input, cotangent, weight, log_perm, well_cells.reshape(1, -1), well_rates.T,
        inject_gain, point_weight, point_bias.reshape(1, -1),
        *[jnp.asarray(table[n]) for n in TABLE_ORDER],
    )
    grad_input, grad_spec, grad_perm = pl.pallas_call(
        hand_over,
        out_shape=results,
        in_specs=[hbm] * 3,
        out_specs=(hbm, hbm, hbm),
        scratch_shapes=[pltpu.VMEM(r.shape, r.dtype) for r in results]
        + [pltpu.SemaphoreType.DMA((7,)), pltpu.SemaphoreType.DMA((7,))],
        compiler_params=pltpu.CompilerParams(vmem_limit_bytes=56 * 1024 * 1024),
    )(*done)
    grad_spec = jnp.transpose(grad_spec.reshape(RL, ML, 2, C * C), (2, 0, 1, 3))
    return grad_input, grad_spec, grad_perm


def solution(mesh):
    return jax.shard_map(
        on_device,
        mesh=mesh,
        in_specs=(
            P(None, "gx", "gy", None),
            P(None, "gx", "gy", None),
            P("gx", "gy", None),
            P(),
            P(),
            P(),
            P(None, "gy", "gx", None),
            P(),
            P(),
        ),
        out_specs=(P(None, "gx", "gy", None), P(None, "gy", "gx", None), P("gx", "gy", None)),
        check_vma=False,
    )
```

```python
import math

import jax
import jax.numpy as jnp
import ml_dtypes
import numpy as np
from jax import lax
from jax.experimental import pallas as pl
from jax.experimental.pallas import tpu as pltpu
from jax.sharding import PartitionSpec as P

C = 20
NX, NY, NZ, NT = 128, 128, 64, 16
MX, MY, MZ, MT = 24, 24, 24, 6
GX, GY = 16, 32
XL, YL = NX // GX, NY // GY
ML = MZ * MT // GX
RL = MX * MY // GY
ZT = NZ * NT
CY = C * YL
NMODE = 2 * MZ * MT
NQ = 3
MQ = ML // NQ
LANES = 256
QL = 128
RB = 128
BF = jnp.bfloat16
F32 = jnp.float32
MESH = pl.DeviceIdType.MESH
INV_ROOT_TWO = 1.0 / math.sqrt(2.0)
INV_ROOT_TWO_PI = 1.0 / math.sqrt(2.0 * math.pi)


def freq(j, n):
    return np.where(j < n // 2, j, j - n)


def lane_of(m, cy):
    if m == 0:
        return cy
    if m == 2:
        return 128 + cy
    return 80 + cy if cy < 48 else 208 + cy - 48


X_FAR = [8] + [o for k in range(7, 0, -1) for o in (k, GX - k)]
Y_FAR = sorted(
    ((dz, dx) for dz in range(8) for dx in range(4) if dz or dx),
    key=lambda d: -(min(d[0], 8 - d[0]) + min(d[1], 4 - d[1])),
)


def first_jx(d):
    return 3 * d // 4


def tables():
    jz, jt = np.divmod(np.arange(MZ * MT), MT)
    k = np.arange(ZT)
    turns = (freq(jz, MZ)[:, None] * (k // NT)[None] * NT + jt[:, None] * (k % NT)[None] * NZ) % ZT
    ang = 2 * np.pi / ZT * turns
    cos, sin = np.cos(ang) / math.sqrt(ZT), np.sin(ang) / math.sqrt(ZT)
    kap = np.where(jt == 0, 1.0, 2.0)[:, None]
    ft = np.stack([cos, -sin], 1)
    inv = np.stack([kap * cos, -kap * sin], 1)

    def by_chunk(a):
        return a.reshape(GX, NQ, MQ, 2, ZT).transpose(1, 0, 2, 3, 4).reshape(NMODE, ZT)

    ft, inv = by_chunk(ft), by_chunk(inv)
    jx = np.arange(MX)
    ang = 2 * np.pi / NX * (freq(jx, MX)[:, None] * np.arange(NX)[None] % NX)
    cx = (np.cos(ang) / math.sqrt(NX)).reshape(MX, GX, XL)
    sx = (np.sin(ang) / math.sqrt(NX)).reshape(MX, GX, XL)
    wx = np.zeros((MX, 2, GX, 2, XL))
    wx[:, 0, :, 0], wx[:, 0, :, 1] = cx, sx
    wx[:, 1, :, 1], wx[:, 1, :, 0] = cx, -sx
    wx = wx.reshape(2 * MX, 2 * NX)
    xi = np.zeros((2 * NX, 128))
    xi[:, : 2 * MX] = wx.T
    perm = np.zeros((LANES, 2 * QL))
    for m in range(MQ):
        for c in range(C):
            for y in range(YL):
                perm[lane_of(m, c * YL + y), y * 64 + m * C + c] = 1
    pick = np.zeros((GY, 2, 2, 2, 2, MX, 2))
    for d in range(GY):
        for s in range(2):
            if s == 1 and d % 4 in (0, 3):
                continue
            for y in range(2):
                for p in range(2):
                    pick[d, y, s, p, y, first_jx(d) + s, p] = 1
    pick = pick.reshape(GY * 8, MX * 4)
    pick_pad = np.zeros((GY * 8, 128))
    pick_pad[:, : MX * 4] = pick
    vc = np.zeros((GY, RL, 2, GY, YL, 2, 2))
    for d in range(GY):
        for i in range(RL):
            a, b = divmod(d * RL + i, MY)
            ang = 2 * np.pi / NY * (int(freq(np.array(b), MY)) * np.arange(NY) % NY)
            cy = (np.cos(ang) / math.sqrt(NY)).reshape(GY, YL)
            sy = (np.sin(ang) / math.sqrt(NY)).reshape(GY, YL)
            s = a - first_jx(d)
            vc[d, i, 0, :, :, s, 0], vc[d, i, 0, :, :, s, 1] = cy, sy
            vc[d, i, 1, :, :, s, 1], vc[d, i, 1, :, :, s, 0] = cy, -sy
    vc = vc.reshape(GY, 2 * RL, GY, 2, 2, 4).transpose(0, 4, 1, 2, 3, 5)
    vc = vc.reshape(GY, 2, 2 * RL, GY * 8)
    v_pad = np.zeros((GY, 2, 48, GY * 8))
    v_pad[:, :, : 2 * RL] = vc
    v_pad = v_pad.reshape(GY, 96, GY * 8)
    u_pad = np.zeros((GY, GY * 8, 128))
    u_pad[:, :, :96] = v_pad.transpose(0, 2, 1)
    rep = np.zeros((6, RB, 128))
    forms = [
        ((0, 1), (1, -1)),
        ((1, 1), (0, 1)),
        ((0, 1), (1, 1)),
        ((1, 1), (0, -1)),
        ((0, 1), (0, 1)),
        ((1, 1), (1, 1)),
    ]
    back = np.zeros((48, 2, RB))
    mask = np.zeros((RB, QL))
    kmask = np.zeros((2, RB, QL))
    for r in range(RL):
        for m in range(MQ):
            for p in range(2):
                row = (r * MQ + m) * 2 + p
                for f, form in enumerate(forms):
                    rep[f, row, 2 * r + form[p][0]] = form[p][1]
                back[2 * r, 0, row] = 1
                back[2 * r + 1, 1, row] = 1
                mask[row, m * C : (m + 1) * C] = 1
                for g in range(2):
                    kmask[g, row, m * C : (m + 1) * C] = 1 if (MQ * g + m) % MT == 0 else 2
    spread = np.zeros((2, QL, 512))
    for m in range(MQ):
        for c in range(C):
            for o in range(C):
                spread[0, m * C + c, c * C + o] = 1
                spread[1, m * C + o, c * C + o] = 1
    cell = np.zeros((XL, C, YL, XL, YL))
    for x in range(XL):
        for y in range(YL):
            cell[x, :, y, x, y] = 1
    cell = cell.reshape(XL * CY, XL * YL)
    chan = np.zeros((CY, C))
    chan[np.arange(CY), np.arange(CY) // YL] = 1
    chan_t = np.zeros((C, 128))
    chan_t[:, :CY] = chan.T
    same_y = np.zeros((CY, 128))
    same_y[:, :CY] = np.arange(CY)[:, None] % YL == np.arange(CY)[None] % YL
    ztrep = np.zeros((2, NZ + NT, ZT))
    ztrep[:, k // NT, k] = 1
    ztrep[:, NZ + k % NT, k] = 1
    ztrep = ztrep.reshape(2 * (NZ + NT), ZT)
    zsum = np.zeros((ZT, 128))
    zsum[k, k // NT] = 1
    out = dict(
        ft=ft, inv=inv, wx=wx, xi=xi, perm=perm, perm_t=perm.T, pick=pick_pad, sel=pick.T,
        v=v_pad, u=u_pad, rep=rep.reshape(6 * RB, 128), back=back.reshape(48, 2 * RB),
        mask=mask, kmask=kmask, spread1=spread[0], spread2=spread[1],
        sum1=spread[1].T, sum2=spread[0].T, cell=cell, chan=chan, chan_t=chan_t,
        same_y=same_y, ztrep=ztrep, zsum=zsum,
    )
    return {n: np.ascontiguousarray(a).astype(ml_dtypes.bfloat16) for n, a in out.items()}


TABLE_ORDER = (
    "cell", "chan", "ztrep", "ft", "chan_t", "same_y", "wx", "perm", "pick", "v", "rep", "mask",
    "spread1", "sum1", "back", "u", "sel", "perm_t", "xi", "inv", "kmask", "spread2", "sum2", "zsum",
)
OWN = ("v", "u")


def dot(a, b):
    return lax.dot_general(a, b, (((1,), (0,)), ((), ())), preferred_element_type=F32)


def dot_nt(a, b):
    return lax.dot_general(a, b, (((1,), (1,)), ((), ())), preferred_element_type=F32)


def dot_tn(a, b):
    return lax.dot_general(a, b, (((0,), (0,)), ((), ())), preferred_element_type=F32)


def gelu_slope(v):
    a = jnp.abs(v) * INV_ROOT_TWO
    t = 1.0 / (1.0 + 0.3275911 * a)
    poly = t * (
        0.254829592
        + t * (-0.284496736 + t * (1.421413741 + t * (-1.453152027 + t * 1.061405429)))
    )
    e = jnp.exp(-0.5 * v * v)
    tail = 0.5 * poly * e
    return jnp.where(v >= 0, 1.0 - tail, tail) + v * e * INV_ROOT_TWO_PI


def split(a):
    hi = a.astype(BF)
    return hi, (a - hi.astype(F32)).astype(BF)


def kernel(*refs):
    names = TABLE_ORDER
    (x_hbm, cot_hbm, w_hbm, perm_ref, cells_ref, rates_ref, gain_ref, pw_ref, bias_ref) = refs[:9]
    hbm = dict(zip(names, refs[9 : 9 + len(names)]))
    pos = 9 + len(names)
    out_hbm, gs_hbm, gp_ref = refs[pos : pos + 3]
    pos += 3
    (
        x_v, cot_v, w_v, out_v, gs_v, lbf, base, cotf, wf, perm_s, stage, stage2, e00, e11, grad, spec_in,
        gxs, gxr, gys, gyr, gx_ss, gx_rs, gy_ss, gy_rs, in_sem, tab_sem, out_sem,
    ) = refs[pos : pos + 27]
    tab = dict(zip(names, refs[pos + 27 :]))
    gx = lax.axis_index("gx")
    gy = lax.axis_index("gy")

    def tab_copy(i):
        n = names[i]
        src = hbm[n]
        if n in OWN:
            src = src.at[gy]
        return pltpu.make_async_copy(src, tab[n], tab_sem.at[i])

    waited = set()

    def need(*wanted):
        for n in wanted:
            if n not in waited:
                waited.add(n)
                tab_copy(names.index(n)).wait()
        got = tuple(tab[n][...] for n in wanted)
        return got if len(got) > 1 else got[0]

    def x_in(x):
        part = pl.ds(x, 2)
        return pltpu.make_async_copy(x_hbm.at[:, part], x_v.at[:, part], in_sem.at[3 + x // 2])

    cot_in = pltpu.make_async_copy(cot_hbm, cot_v, in_sem.at[1])
    w_in = pltpu.make_async_copy(w_hbm, w_v, in_sem.at[2])
    for i in range(3):
        tab_copy(i).start()
    x_in(0).start()
    tab_copy(3).start()
    for x in range(2, XL, 2):
        x_in(x).start()
    barrier = pltpu.get_barrier_semaphore()

    @pl.loop(1, GX)
    def _(o):
        pl.semaphore_signal(
            barrier, inc=1, device_id=(lax.rem(gx + o, GX), gy), device_id_type=MESH
        )

    @pl.loop(1, GY)
    def _(o):
        pl.semaphore_signal(
            barrier, inc=1, device_id=(gx, lax.rem(gy + o, GY)), device_id_type=MESH
        )

    def gx_copy(step, q, o, landing):
        peer = lax.rem(gx + o, GX)
        return pltpu.make_async_remote_copy(
            src_ref=gxs.at[step * NQ + q, peer],
            dst_ref=gxr.at[step * NQ + q, landing],
            send_sem=gx_ss.at[step * NQ + q],
            recv_sem=gx_rs.at[step * NQ + q],
            device_id=(peer, gy),
            device_id_type=MESH,
        )

    def gy_copy(step, q, o, landing):
        peer = lax.rem(gy // 4 + o[0], 8) * 4 + lax.rem(gy + o[1], 4)
        return pltpu.make_async_remote_copy(
            src_ref=gys.at[step * NQ + q, peer],
            dst_ref=gyr.at[step * NQ + q, landing],
            send_sem=gy_ss.at[step * NQ + q],
            recv_sem=gy_rs.at[step * NQ + q],
            device_id=(gx, peer),
            device_id_type=MESH,
        )

    def all_blocks(buf, sem, i, peers):
        blocks = buf.at[i, pl.ds(0, peers - 1)]
        return pltpu.make_async_copy(blocks, blocks, sem.at[i])

    def gx_wait(step, q):
        all_blocks(gxr, gx_rs, step * NQ + q, GX).wait()

    def gy_wait(step, q):
        all_blocks(gyr, gy_rs, step * NQ + q, GY).wait()

    def gy_send(step, q):
        for o in Y_FAR:
            gy_copy(step, q, o, gy).start()
        gyr[step * NQ + q, gy] = gys[step * NQ + q, gy]

    lane = lax.broadcasted_iota(jnp.int32, (16, 128), 1)

    chan = need("chan")
    chan_f = chan.astype(F32)
    gain0 = jnp.sum(chan_f * gain_ref[0:1, :], axis=1, keepdims=True)
    gain1 = jnp.sum(chan_f * gain_ref[1:2, :], axis=1, keepdims=True)
    bias = jnp.sum(chan_f * bias_ref[...], axis=1, keepdims=True)

    for x in range(XL):
        perm_s[x * YL : (x + 1) * YL, :] = perm_ref[x]
    cell = need("cell")
    perm_hi, perm_lo = split(perm_s[...])
    col = lax.broadcasted_iota(jnp.int32, (XL * YL, 32), 0)
    cell_id = (gx * XL + col // YL) * NY + gy * YL + col % YL
    hits = (cells_ref[...] == cell_id).astype(BF)
    inflow = 0.5 * dot_nt(hits, rates_ref[...].astype(F32).astype(BF))
    perm_rows = dot(cell, perm_hi) + dot(cell, perm_lo)
    flow_rows = dot(cell, inflow.astype(BF))
    ztrep = need("ztrep")

    def spread_rows(src, x, dst):
        for c in range(C):
            dst[c * YL : (c + 1) * YL, :] = src[c, x].astype(F32)

    def zt_pair(field, x):
        z = dot_nt(need("ft"), field[x : x + 2].reshape(256, ZT))
        stage[:, x, :] = z[:, :128]
        stage[:, x + 1, :] = z[:, 128:]

    parts = jnp.concatenate(
        [
            jnp.concatenate([gain0] * XL, axis=0) * perm_rows,
            jnp.concatenate([gain1] * XL, axis=0) * flow_rows,
        ],
        axis=1,
    )
    parts = jnp.concatenate(split(parts), axis=1)
    for x in range(XL):
        if x % 2 == 0:
            x_in(x).wait()
        added = dot(parts[x * CY : (x + 1) * CY], ztrep)
        spread_rows(x_v, x, base.at[x])
        total = (base[x] + added).astype(BF)
        lbf[x, :CY] = total
        lbf[x, CY:] = total[:48]
        if x % 2:
            zt_pair(lbf, x - 1)
    w_in.start()
    for i in range(4, 10):
        tab_copy(i).start()
    cot_in.start()
    for i in range(10, len(names)):
        tab_copy(i).start()

    def pack(q, peer, into):
        row = (q * GX + peer) * MQ * 2
        blk = [stage[pl.ds(row + 2 * m, 2)].reshape(16, 128) for m in range(MQ)]
        into[:, :128] = jnp.where(lane < 80, blk[0], blk[1]).astype(BF)
        into[:, 128:] = jnp.where(lane < 80, blk[2], pltpu.roll(blk[1], 32, 1)).astype(BF)

    def gx_send(step, q):
        for o in X_FAR:
            gx_copy(step, q, o, gx).start()
        gxr[step * NQ + q, gx] = gxs[step * NQ + q, gx]

    def gx_send_packed(step):
        for q in range(NQ):
            for peer in range(GX):
                pack(q, peer, gxs.at[step * NQ + q, peer])
            gx_send(step, q)

    def to_owners(step, q):
        gx_wait(step, q)
        got = gxr[step * NQ + q].reshape(256, LANES)
        xs = dot(need("wx"), got).astype(BF)
        ys = dot(xs, need("perm")).astype(BF)
        rows = jnp.concatenate([ys[:, :QL], ys[:, QL:], jnp.zeros((32, QL), BF)], axis=0)
        gys[step * NQ + q] = dot(need("pick"), rows).reshape(GY, 8, QL).astype(BF)
        gy_send(step, q)

    def gy_rows(step, q):
        gy_wait(step, q)
        return gyr[step * NQ + q].astype(F32).reshape(GY * 8, QL).astype(BF)

    def spectrum(step, q):
        both = dot(need("v"), gy_rows(step, q))
        spec = (both[:48] + pltpu.roll(both[48:], 64, 1)).astype(BF)
        return jnp.concatenate([spec, jnp.zeros((80, QL), BF)], axis=0)

    def expand(spec, forms, mask, spread):
        rep = tab["rep"][forms * RB : (forms + 2) * RB, :]
        rows = dot(rep, spec).astype(BF) * jnp.concatenate([mask, mask], axis=0)
        return dot(rows, spread)

    def mix(step, q, terms, summing):
        mask = need("mask")
        wide = jnp.concatenate([wf[q], wf[q]], axis=0)
        rows = dot((terms * wide).astype(BF), summing).astype(BF)
        rows = rows * jnp.concatenate([mask, mask], axis=0)
        mixed = dot(need("back"), rows)
        pair = jnp.concatenate([mixed, pltpu.roll(mixed, 64, 1), jnp.zeros((32, QL), F32)], axis=0)
        gys[step * NQ + q] = dot(need("u"), pair.astype(BF)).reshape(GY, 8, QL).astype(BF)
        gy_send(step, q)

    def to_columns(step, q):
        ys = dot(need("sel"), gy_rows(step, q)).astype(BF)
        wide = jnp.concatenate([ys[:48], ys[48:]], axis=1)
        xs = dot(wide, need("perm_t")).astype(BF)
        xs = jnp.concatenate([xs, jnp.zeros((80, LANES), BF)], axis=0)
        gxs[step * NQ + q] = dot(need("xi"), xs).astype(BF).reshape(GX, 16, LANES)
        gx_send(step, q)

    def unpack(step, q, src):
        got = [
            gxr[step * NQ + q, src, :, t * 128 : (t + 1) * 128].astype(F32) for t in range(2)
        ]
        middle = jnp.where(lane < 48, pltpu.roll(got[0], 48, 1), pltpu.roll(got[1], 96, 1))
        row = (q * GX + src) * MQ * 2
        for m, v in enumerate((got[0], middle, got[1])):
            stage2[row + 2 * m : row + 2 * m + 2] = v.reshape(2, 8, 128)

    def receive_images(step, q):
        gx_wait(step, q)
        for src in range(GX):
            unpack(step, q, src)

    def image_of(q, x):
        rows = slice(q * 2 * ML * GX // NQ, (q + 1) * 2 * ML * GX // NQ)
        return dot_tn(stage2[rows, x, :].astype(BF), need("inv")[rows])[:CY]

    def exchange(step, middle, beside):
        beside(0)
        for q in range(NQ):
            to_owners(step, q)
        beside(1)
        for q in range(NQ):
            middle(q)
        beside(2)
        for q in range(NQ):
            to_columns(step + 1, q)
        beside(3)
        for q in range(NQ):
            receive_images(step + 1, q)
            if q < NQ - 1:
                for x in range(XL):
                    base[x] += image_of(q, x)

    pl.semaphore_wait(barrier, GX + GY - 2)
    gx_send_packed(0)

    chan_t, same_y = need("chan_t", "same_y")
    pw = pw_ref[...]
    pw_fwd = (dot(dot_nt(chan, pw).astype(BF), chan_t) * same_y.astype(F32)).astype(BF)
    pw_bwd = (dot(dot(chan, pw).astype(BF), chan_t) * same_y.astype(F32)).astype(BF)

    def forward_middle(q):
        spec = spectrum(0, q)
        spec_in[q] = spec
        mix(1, q, expand(spec, 0, need("mask"), need("spread1")), need("sum1"))

    def forward_beside(slot):
        if slot == 0:
            need("rep")
            w_in.wait()
            wf[...] = jnp.zeros((NQ, RB, 512), F32)
            for r in range(RL):
                for m in range(ML):
                    q, row = m // MQ, (r * MQ + m % MQ) * 2
                    wf[q, row : row + 2, :400] = w_v[r * ML + m].astype(F32)
            for x in range(XL):
                base[x] = dot(pw_fwd, lbf[x]) + bias
            cot_in.wait()
            for x in range(XL):
                spread_rows(cot_v, x, cotf.at[x])
        if slot == 3:
            need("kmask")
            for q in range(NQ):
                kmask = tab["kmask"][lax.rem(gx + q, 2)]
                both = expand(spec_in[q], 4, kmask, need("spread1"))
                e00[q] = both[:RB]
                e11[q] = both[RB:]

    exchange(0, forward_middle, forward_beside)
    for x in range(XL):
        pre = base[x] + image_of(NQ - 1, x)
        delta = (cotf[x] * gelu_slope(pre)).astype(BF)
        lbf[x, :CY] = delta
        lbf[x, CY:] = delta[:48]
        if x % 2:
            zt_pair(lbf, x - 1)

    gx_send_packed(2)
    gs_out = pltpu.make_async_copy(gs_v, gs_hbm, out_sem.at[XL])

    def backward_middle(q):
        terms = expand(spectrum(2, q), 2, need("mask"), need("spread2"))
        mix(3, q, terms, need("sum2"))
        grad[q] = terms[:RB] * e00[q] + terms[RB:] * e11[q]

    def backward_beside(slot):
        if slot == 0:
            for x in range(XL):
                base[x] = dot(pw_bwd, lbf[x])
        if slot == 3:
            for r in range(RL):
                for m in range(ML):
                    q, row = m // MQ, (r * MQ + m % MQ) * 2
                    gs_v[r * ML + m] = grad[q, row : row + 2, :400]
            gs_out.start()

    exchange(2, backward_middle, backward_beside)
    zsum = need("zsum")

    def out_copy(x):
        return pltpu.make_async_copy(out_v.at[:, x], out_hbm.at[:, x], out_sem.at[x])

    for x in range(XL):
        field = base[x] + image_of(NQ - 1, x)
        cotf[x] = field
        for c in range(C):
            out_v[c, x] = cotf[x, c * YL : (c + 1) * YL, :].astype(BF)
        out_copy(x).start()
        hi, lo = split(field * gain0)
        zs = dot(hi, zsum) + dot(lo, zsum)
        acc = zs[:8]
        for c in range(1, CY // 8):
            acc = acc + zs[8 * c : 8 * c + 8]
        gp_ref[x] = (acc[:4] + acc[4:])[:, :NZ]

    for x in range(XL):
        out_copy(x).wait()
    gs_out.wait()
    for i in range(4 * NQ):
        all_blocks(gxs, gx_ss, i, GX).wait()
        all_blocks(gys, gy_ss, i, GY).wait()


def hand_over(*refs):
    given, result, held, (in_sem, out_sem) = refs[:3], refs[3:6], refs[6:9], refs[9:]
    part = C // 5
    places = [(0, pl.ds(i * part, part)) for i in range(5)] + [(1, slice(None)), (2, slice(None))]
    ins, outs = [], []
    for i, (a, at) in enumerate(places):
        ins.append(pltpu.make_async_copy(given[a].at[at], held[a].at[at], in_sem.at[i]))
        outs.append(pltpu.make_async_copy(held[a].at[at], result[a].at[at], out_sem.at[i]))
    for c in ins:
        c.start()
    for a, b in zip(ins, outs):
        a.wait()
        b.start()
    for c in outs:
        c.wait()


def on_device(
    layer_input, cotangent, log_perm, well_cells, well_rates, inject_gain, spectral_weight,
    point_weight, point_bias,
):
    table = tables()
    weight = jnp.transpose(spectral_weight, (1, 2, 0, 3)).reshape(RL * ML, 2, C * C)
    hbm = pl.BlockSpec(memory_space=pl.ANY)
    vmem = pl.BlockSpec(memory_space=pltpu.VMEM)
    scratch = [
        pltpu.VMEM((C, XL, YL, ZT), BF),
        pltpu.VMEM((C, XL, YL, ZT), BF),
        pltpu.VMEM((RL * ML, 2, C * C), BF),
        pltpu.VMEM((C, XL, YL, ZT), BF),
        pltpu.VMEM((RL * ML, 2, C * C), F32),
        pltpu.VMEM((XL, 128, ZT), BF),
        pltpu.VMEM((XL, CY, ZT), F32),
        pltpu.VMEM((XL, CY, ZT), F32),
        pltpu.VMEM((NQ, RB, 512), F32),
        pltpu.VMEM((XL * YL, NZ), F32),
        pltpu.VMEM((NMODE, XL, 128), F32),
        pltpu.VMEM((NMODE, XL, 128), F32),
        pltpu.VMEM((NQ, RB, 512), F32),
        pltpu.VMEM((NQ, RB, 512), F32),
        pltpu.VMEM((NQ, RB, 512), F32),
        pltpu.VMEM((NQ, QL, QL), BF),
        pltpu.VMEM((4 * NQ, GX, 16, LANES), BF),
        pltpu.VMEM((4 * NQ, GX, 16, LANES), BF),
        pltpu.VMEM((4 * NQ, GY, 8, QL), BF),
        pltpu.VMEM((4 * NQ, GY, 8, QL), BF),
        pltpu.SemaphoreType.DMA((4 * NQ,)),
        pltpu.SemaphoreType.DMA((4 * NQ,)),
        pltpu.SemaphoreType.DMA((4 * NQ,)),
        pltpu.SemaphoreType.DMA((4 * NQ,)),
        pltpu.SemaphoreType.DMA((3 + XL // 2,)),
        pltpu.SemaphoreType.DMA((len(TABLE_ORDER),)),
        pltpu.SemaphoreType.DMA((XL + 1,)),
    ]
    for n in TABLE_ORDER:
        shape = table[n].shape[1:] if n in OWN else table[n].shape
        scratch.append(pltpu.VMEM(shape, BF))
    results = (
        jax.ShapeDtypeStruct((C, XL, YL, ZT), BF),
        jax.ShapeDtypeStruct((RL * ML, 2, C * C), F32),
        jax.ShapeDtypeStruct((XL, YL, NZ), F32),
    )
    done = pl.pallas_call(
        kernel,
        out_shape=results,
        in_specs=[hbm] * 3 + [vmem] * 6 + [hbm] * len(TABLE_ORDER),
        out_specs=(hbm, hbm, vmem),
        scratch_shapes=scratch,
        compiler_params=pltpu.CompilerParams(
            collective_id=0, has_side_effects=True, vmem_limit_bytes=56 * 1024 * 1024
        ),
    )(
        layer_input, cotangent, weight, log_perm, well_cells.reshape(1, -1), well_rates.T,
        inject_gain, point_weight, point_bias.reshape(1, -1),
        *[jnp.asarray(table[n]) for n in TABLE_ORDER],
    )
    grad_input, grad_spec, grad_perm = pl.pallas_call(
        hand_over,
        out_shape=results,
        in_specs=[hbm] * 3,
        out_specs=(hbm, hbm, hbm),
        scratch_shapes=[pltpu.VMEM(r.shape, r.dtype) for r in results]
        + [pltpu.SemaphoreType.DMA((7,)), pltpu.SemaphoreType.DMA((7,))],
        compiler_params=pltpu.CompilerParams(vmem_limit_bytes=56 * 1024 * 1024),
    )(*done)
    grad_spec = jnp.transpose(grad_spec.reshape(RL, ML, 2, C * C), (2, 0, 1, 3))
    return grad_input, grad_spec, grad_perm


def solution(mesh):
    return jax.shard_map(
        on_device,
        mesh=mesh,
        in_specs=(
            P(None, "gx", "gy", None),
            P(None, "gx", "gy", None),
            P("gx", "gy", None),
            P(),
            P(),
            P(),
            P(None, "gy", "gx", None),
            P(),
            P(),
        ),
        out_specs=(P(None, "gx", "gy", None), P(None, "gy", "gx", None), P("gx", "gy", None)),
        check_vma=False,
    )
```

```python
import math

import jax
import jax.numpy as jnp
import ml_dtypes
import numpy as np
from jax import lax
from jax.experimental import pallas as pl
from jax.experimental.pallas import tpu as pltpu
from jax.sharding import PartitionSpec as P

C = 20
NX, NY, NZ, NT = 128, 128, 64, 16
MX, MY, MZ, MT = 24, 24, 24, 6
GX, GY = 16, 32
XL, YL = NX // GX, NY // GY
ML = MZ * MT // GX
RL = MX * MY // GY
ZT = NZ * NT
CY = C * YL
NMODE = 2 * MZ * MT
NQ = 3
MQ = ML // NQ
LANES = 256
QL = 128
RB = 128
BF = jnp.bfloat16
F32 = jnp.float32
MESH = pl.DeviceIdType.MESH
INV_ROOT_TWO = 1.0 / math.sqrt(2.0)
INV_ROOT_TWO_PI = 1.0 / math.sqrt(2.0 * math.pi)


def freq(j, n):
    return np.where(j < n // 2, j, j - n)


def lane_of(m, cy):
    if m == 0:
        return cy
    if m == 2:
        return 128 + cy
    return 80 + cy if cy < 48 else 208 + cy - 48


X_FAR = [8] + [o for k in range(7, 0, -1) for o in (k, GX - k)]
Y_FAR = sorted(
    ((dz, dx) for dz in range(8) for dx in range(4) if dz or dx),
    key=lambda d: -(min(d[0], 8 - d[0]) + min(d[1], 4 - d[1])),
)


def first_jx(d):
    return 3 * d // 4


def tables():
    jz, jt = np.divmod(np.arange(MZ * MT), MT)
    k = np.arange(ZT)
    turns = (freq(jz, MZ)[:, None] * (k // NT)[None] * NT + jt[:, None] * (k % NT)[None] * NZ) % ZT
    ang = 2 * np.pi / ZT * turns
    cos, sin = np.cos(ang) / math.sqrt(ZT), np.sin(ang) / math.sqrt(ZT)
    kap = np.where(jt == 0, 1.0, 2.0)[:, None]
    ft = np.stack([cos, -sin], 1)
    inv = np.stack([kap * cos, -kap * sin], 1)

    def by_chunk(a):
        return a.reshape(GX, NQ, MQ, 2, ZT).transpose(1, 0, 2, 3, 4).reshape(NMODE, ZT)

    ft, inv = by_chunk(ft), by_chunk(inv)
    jx = np.arange(MX)
    ang = 2 * np.pi / NX * (freq(jx, MX)[:, None] * np.arange(NX)[None] % NX)
    cx = (np.cos(ang) / math.sqrt(NX)).reshape(MX, GX, XL)
    sx = (np.sin(ang) / math.sqrt(NX)).reshape(MX, GX, XL)
    wx = np.zeros((MX, 2, GX, 2, XL))
    wx[:, 0, :, 0], wx[:, 0, :, 1] = cx, sx
    wx[:, 1, :, 1], wx[:, 1, :, 0] = cx, -sx
    wx = wx.reshape(2 * MX, 2 * NX)
    xi = np.zeros((2 * NX, 128))
    xi[:, : 2 * MX] = wx.T
    perm = np.zeros((LANES, 2 * QL))
    for m in range(MQ):
        for c in range(C):
            for y in range(YL):
                perm[lane_of(m, c * YL + y), y * 64 + m * C + c] = 1
    pick = np.zeros((GY, 2, 2, 2, 2, MX, 2))
    for d in range(GY):
        for s in range(2):
            if s == 1 and d % 4 in (0, 3):
                continue
            for y in range(2):
                for p in range(2):
                    pick[d, y, s, p, y, first_jx(d) + s, p] = 1
    pick = pick.reshape(GY * 8, MX * 4)
    pick_pad = np.zeros((GY * 8, 128))
    pick_pad[:, : MX * 4] = pick
    vc = np.zeros((GY, RL, 2, GY, YL, 2, 2))
    for d in range(GY):
        for i in range(RL):
            a, b = divmod(d * RL + i, MY)
            ang = 2 * np.pi / NY * (int(freq(np.array(b), MY)) * np.arange(NY) % NY)
            cy = (np.cos(ang) / math.sqrt(NY)).reshape(GY, YL)
            sy = (np.sin(ang) / math.sqrt(NY)).reshape(GY, YL)
            s = a - first_jx(d)
            vc[d, i, 0, :, :, s, 0], vc[d, i, 0, :, :, s, 1] = cy, sy
            vc[d, i, 1, :, :, s, 1], vc[d, i, 1, :, :, s, 0] = cy, -sy
    vc = vc.reshape(GY, 2 * RL, GY, 2, 2, 4).transpose(0, 4, 1, 2, 3, 5)
    vc = vc.reshape(GY, 2, 2 * RL, GY * 8)
    v_pad = np.zeros((GY, 2, 48, GY * 8))
    v_pad[:, :, : 2 * RL] = vc
    v_pad = v_pad.reshape(GY, 96, GY * 8)
    u_pad = np.zeros((GY, GY * 8, 128))
    u_pad[:, :, :96] = v_pad.transpose(0, 2, 1)
    rep = np.zeros((6, RB, 128))
    forms = [
        ((0, 1), (1, -1)),
        ((1, 1), (0, 1)),
        ((0, 1), (1, 1)),
        ((1, 1), (0, -1)),
        ((0, 1), (0, 1)),
        ((1, 1), (1, 1)),
    ]
    back = np.zeros((48, 2, RB))
    mask = np.zeros((RB, QL))
    kmask = np.zeros((2, RB, QL))
    for r in range(RL):
        for m in range(MQ):
            for p in range(2):
                row = (r * MQ + m) * 2 + p
                for f, form in enumerate(forms):
                    rep[f, row, 2 * r + form[p][0]] = form[p][1]
                back[2 * r, 0, row] = 1
                back[2 * r + 1, 1, row] = 1
                mask[row, m * C : (m + 1) * C] = 1
                for g in range(2):
                    kmask[g, row, m * C : (m + 1) * C] = 1 if (MQ * g + m) % MT == 0 else 2
    spread = np.zeros((2, QL, 512))
    for m in range(MQ):
        for c in range(C):
            for o in range(C):
                spread[0, m * C + c, c * C + o] = 1
                spread[1, m * C + o, c * C + o] = 1
    cell = np.zeros((XL, C, YL, XL, YL))
    for x in range(XL):
        for y in range(YL):
            cell[x, :, y, x, y] = 1
    cell = cell.reshape(XL * CY, XL * YL)
    chan = np.zeros((CY, C))
    chan[np.arange(CY), np.arange(CY) // YL] = 1
    chan_t = np.zeros((C, 128))
    chan_t[:, :CY] = chan.T
    same_y = np.zeros((CY, 128))
    same_y[:, :CY] = np.arange(CY)[:, None] % YL == np.arange(CY)[None] % YL
    ztrep = np.zeros((2, NZ + NT, ZT))
    ztrep[:, k // NT, k] = 1
    ztrep[:, NZ + k % NT, k] = 1
    ztrep = ztrep.reshape(2 * (NZ + NT), ZT)
    zsum = np.zeros((ZT, 128))
    zsum[k, k // NT] = 1
    out = dict(
        ft=ft, inv=inv, wx=wx, xi=xi, perm=perm, perm_t=perm.T, pick=pick_pad, sel=pick.T,
        v=v_pad, u=u_pad, rep=rep.reshape(6 * RB, 128), back=back.reshape(48, 2 * RB),
        mask=mask, kmask=kmask, spread1=spread[0], spread2=spread[1],
        sum1=spread[1].T, sum2=spread[0].T, cell=cell, chan=chan, chan_t=chan_t,
        same_y=same_y, ztrep=ztrep, zsum=zsum,
    )
    return {n: np.ascontiguousarray(a).astype(ml_dtypes.bfloat16) for n, a in out.items()}


TABLE_ORDER = (
    "cell", "chan", "ztrep", "ft", "chan_t", "same_y", "wx", "perm", "pick", "v", "rep", "mask",
    "spread1", "sum1", "back", "u", "sel", "perm_t", "xi", "inv", "kmask", "spread2", "sum2", "zsum",
)
OWN = ("v", "u")


def dot(a, b):
    return lax.dot_general(a, b, (((1,), (0,)), ((), ())), preferred_element_type=F32)


def dot_nt(a, b):
    return lax.dot_general(a, b, (((1,), (1,)), ((), ())), preferred_element_type=F32)


def dot_tn(a, b):
    return lax.dot_general(a, b, (((0,), (0,)), ((), ())), preferred_element_type=F32)


def gelu_slope(v):
    a = jnp.abs(v) * INV_ROOT_TWO
    t = 1.0 / (1.0 + 0.3275911 * a)
    poly = t * (
        0.254829592
        + t * (-0.284496736 + t * (1.421413741 + t * (-1.453152027 + t * 1.061405429)))
    )
    e = jnp.exp(-0.5 * v * v)
    tail = 0.5 * poly * e
    return jnp.where(v >= 0, 1.0 - tail, tail) + v * e * INV_ROOT_TWO_PI


def split(a):
    hi = a.astype(BF)
    return hi, (a - hi.astype(F32)).astype(BF)


def kernel(*refs):
    names = TABLE_ORDER
    x_hbm, cot_hbm, w_hbm = refs[:3]
    small_hbm = refs[3:9]
    hbm = dict(zip(names, refs[9 : 9 + len(names)]))
    pos = 9 + len(names)
    out_hbm, gs_hbm, gp_hbm = refs[pos : pos + 3]
    pos += 3
    (
        x_v, cot_v, w_v, out_v, gs_v, lbf, base, cotf, wf, perm_s, stage, stage2, e00, e11, grad, spec_in,
        gxs, gxr, gys, gyr, gx_ss, gx_rs, gy_ss, gy_rs, in_sem, tab_sem, out_sem,
        gp_ref, perm_ref, cells_ref, rates_ref, gain_ref, pw_ref, bias_ref, small_sem,
    ) = refs[pos : pos + 35]
    small = (perm_ref, cells_ref, rates_ref, gain_ref, pw_ref, bias_ref)
    tab = dict(zip(names, refs[pos + 35 :]))
    gx = lax.axis_index("gx")
    gy = lax.axis_index("gy")

    def tab_copy(i):
        n = names[i]
        src = hbm[n]
        if n in OWN:
            src = src.at[gy]
        return pltpu.make_async_copy(src, tab[n], tab_sem.at[i])

    waited = set()

    def need(*wanted):
        for n in wanted:
            if n not in waited:
                waited.add(n)
                tab_copy(names.index(n)).wait()
        got = tuple(tab[n][...] for n in wanted)
        return got if len(got) > 1 else got[0]

    def x_in(x):
        part = pl.ds(x, 2)
        return pltpu.make_async_copy(x_hbm.at[:, part], x_v.at[:, part], in_sem.at[3 + x // 2])

    cot_in = pltpu.make_async_copy(cot_hbm, cot_v, in_sem.at[1])
    w_in = pltpu.make_async_copy(w_hbm, w_v, in_sem.at[2])
    small_in = [
        pltpu.make_async_copy(a, b, small_sem.at[i])
        for i, (a, b) in enumerate(zip(small_hbm, small))
    ]
    for c in small_in:
        c.start()
    for i in range(3):
        tab_copy(i).start()
    x_in(0).start()
    tab_copy(3).start()
    for x in range(2, XL, 2):
        x_in(x).start()
    barrier = pltpu.get_barrier_semaphore()

    @pl.loop(1, GX)
    def _(o):
        pl.semaphore_signal(
            barrier, inc=1, device_id=(lax.rem(gx + o, GX), gy), device_id_type=MESH
        )

    @pl.loop(1, GY)
    def _(o):
        pl.semaphore_signal(
            barrier, inc=1, device_id=(gx, lax.rem(gy + o, GY)), device_id_type=MESH
        )

    def gx_copy(step, q, o, landing):
        peer = lax.rem(gx + o, GX)
        return pltpu.make_async_remote_copy(
            src_ref=gxs.at[step * NQ + q, peer],
            dst_ref=gxr.at[step * NQ + q, landing],
            send_sem=gx_ss.at[step * NQ + q],
            recv_sem=gx_rs.at[step * NQ + q],
            device_id=(peer, gy),
            device_id_type=MESH,
        )

    def gy_copy(step, q, o, landing):
        peer = lax.rem(gy // 4 + o[0], 8) * 4 + lax.rem(gy + o[1], 4)
        return pltpu.make_async_remote_copy(
            src_ref=gys.at[step * NQ + q, peer],
            dst_ref=gyr.at[step * NQ + q, landing],
            send_sem=gy_ss.at[step * NQ + q],
            recv_sem=gy_rs.at[step * NQ + q],
            device_id=(gx, peer),
            device_id_type=MESH,
        )

    def all_blocks(buf, sem, i, peers):
        blocks = buf.at[i, pl.ds(0, peers - 1)]
        return pltpu.make_async_copy(blocks, blocks, sem.at[i])

    def gx_wait(step, q):
        all_blocks(gxr, gx_rs, step * NQ + q, GX).wait()

    def gy_wait(step, q):
        all_blocks(gyr, gy_rs, step * NQ + q, GY).wait()

    def gy_send(step, q):
        for o in Y_FAR:
            gy_copy(step, q, o, gy).start()
        gyr[step * NQ + q, gy] = gys[step * NQ + q, gy]

    lane = lax.broadcasted_iota(jnp.int32, (16, 128), 1)

    for c in small_in:
        c.wait()
    chan = need("chan")
    chan_f = chan.astype(F32)
    gain0 = jnp.sum(chan_f * gain_ref[0:1, :], axis=1, keepdims=True)
    gain1 = jnp.sum(chan_f * gain_ref[1:2, :], axis=1, keepdims=True)
    bias = jnp.sum(chan_f * bias_ref[...], axis=1, keepdims=True)

    for x in range(XL):
        perm_s[x * YL : (x + 1) * YL, :] = perm_ref[x]
    cell = need("cell")
    perm_hi, perm_lo = split(perm_s[...])
    col = lax.broadcasted_iota(jnp.int32, (XL * YL, 32), 0)
    cell_id = (gx * XL + col // YL) * NY + gy * YL + col % YL
    hits = (cells_ref[...] == cell_id).astype(BF)
    inflow = 0.5 * dot_nt(hits, rates_ref[...].astype(F32).astype(BF))
    perm_rows = dot(cell, perm_hi) + dot(cell, perm_lo)
    flow_rows = dot(cell, inflow.astype(BF))
    ztrep = need("ztrep")

    def spread_rows(src, x, dst):
        for c in range(C):
            dst[c * YL : (c + 1) * YL, :] = src[c, x].astype(F32)

    def zt_pair(field, x):
        z = dot_nt(need("ft"), field[x : x + 2].reshape(256, ZT))
        stage[:, x, :] = z[:, :128]
        stage[:, x + 1, :] = z[:, 128:]

    parts = jnp.concatenate(
        [
            jnp.concatenate([gain0] * XL, axis=0) * perm_rows,
            jnp.concatenate([gain1] * XL, axis=0) * flow_rows,
        ],
        axis=1,
    )
    parts = jnp.concatenate(split(parts), axis=1)
    for x in range(XL):
        if x % 2 == 0:
            x_in(x).wait()
        added = dot(parts[x * CY : (x + 1) * CY], ztrep)
        spread_rows(x_v, x, base.at[x])
        total = (base[x] + added).astype(BF)
        lbf[x, :CY] = total
        lbf[x, CY:] = total[:48]
        if x % 2:
            zt_pair(lbf, x - 1)
    w_in.start()
    for i in range(4, 10):
        tab_copy(i).start()
    cot_in.start()
    for i in range(10, len(names)):
        tab_copy(i).start()

    def pack(q, peer, into):
        row = (q * GX + peer) * MQ * 2
        blk = [stage[pl.ds(row + 2 * m, 2)].reshape(16, 128) for m in range(MQ)]
        into[:, :128] = jnp.where(lane < 80, blk[0], blk[1]).astype(BF)
        into[:, 128:] = jnp.where(lane < 80, blk[2], pltpu.roll(blk[1], 32, 1)).astype(BF)

    def gx_send(step, q):
        for o in X_FAR:
            gx_copy(step, q, o, gx).start()
        gxr[step * NQ + q, gx] = gxs[step * NQ + q, gx]

    def gx_send_packed(step):
        for q in range(NQ):
            for peer in range(GX):
                pack(q, peer, gxs.at[step * NQ + q, peer])
            gx_send(step, q)

    def to_owners(step, q):
        gx_wait(step, q)
        got = gxr[step * NQ + q].reshape(256, LANES)
        xs = dot(need("wx"), got).astype(BF)
        ys = dot(xs, need("perm")).astype(BF)
        rows = jnp.concatenate([ys[:, :QL], ys[:, QL:], jnp.zeros((32, QL), BF)], axis=0)
        gys[step * NQ + q] = dot(need("pick"), rows).reshape(GY, 8, QL).astype(BF)
        gy_send(step, q)

    def gy_rows(step, q):
        gy_wait(step, q)
        return gyr[step * NQ + q].astype(F32).reshape(GY * 8, QL).astype(BF)

    def spectrum(step, q):
        both = dot(need("v"), gy_rows(step, q))
        spec = (both[:48] + pltpu.roll(both[48:], 64, 1)).astype(BF)
        return jnp.concatenate([spec, jnp.zeros((80, QL), BF)], axis=0)

    def expand(spec, forms, mask, spread):
        rep = tab["rep"][forms * RB : (forms + 2) * RB, :]
        rows = dot(rep, spec).astype(BF) * jnp.concatenate([mask, mask], axis=0)
        return dot(rows, spread)

    def mix(step, q, terms, summing):
        mask = need("mask")
        wide = jnp.concatenate([wf[q], wf[q]], axis=0)
        rows = dot((terms * wide).astype(BF), summing).astype(BF)
        rows = rows * jnp.concatenate([mask, mask], axis=0)
        mixed = dot(need("back"), rows)
        pair = jnp.concatenate([mixed, pltpu.roll(mixed, 64, 1), jnp.zeros((32, QL), F32)], axis=0)
        gys[step * NQ + q] = dot(need("u"), pair.astype(BF)).reshape(GY, 8, QL).astype(BF)
        gy_send(step, q)

    def to_columns(step, q):
        ys = dot(need("sel"), gy_rows(step, q)).astype(BF)
        wide = jnp.concatenate([ys[:48], ys[48:]], axis=1)
        xs = dot(wide, need("perm_t")).astype(BF)
        xs = jnp.concatenate([xs, jnp.zeros((80, LANES), BF)], axis=0)
        gxs[step * NQ + q] = dot(need("xi"), xs).astype(BF).reshape(GX, 16, LANES)
        gx_send(step, q)

    def unpack(step, q, src):
        got = [
            gxr[step * NQ + q, src, :, t * 128 : (t + 1) * 128].astype(F32) for t in range(2)
        ]
        middle = jnp.where(lane < 48, pltpu.roll(got[0], 48, 1), pltpu.roll(got[1], 96, 1))
        row = (q * GX + src) * MQ * 2
        for m, v in enumerate((got[0], middle, got[1])):
            stage2[row + 2 * m : row + 2 * m + 2] = v.reshape(2, 8, 128)

    def receive_images(step, q):
        gx_wait(step, q)
        for src in range(GX):
            unpack(step, q, src)

    def image_of(q, x):
        rows = slice(q * 2 * ML * GX // NQ, (q + 1) * 2 * ML * GX // NQ)
        return dot_tn(stage2[rows, x, :].astype(BF), need("inv")[rows])[:CY]

    def exchange(step, middle, beside):
        beside(0)
        for q in range(NQ):
            to_owners(step, q)
        beside(1)
        for q in range(NQ):
            middle(q)
        beside(2)
        for q in range(NQ):
            to_columns(step + 1, q)
        beside(3)
        for q in range(NQ):
            receive_images(step + 1, q)
            if q < NQ - 1:
                for x in range(XL):
                    base[x] += image_of(q, x)

    pl.semaphore_wait(barrier, GX + GY - 2)
    gx_send_packed(0)

    chan_t, same_y = need("chan_t", "same_y")
    pw = pw_ref[...]
    pw_fwd = (dot(dot_nt(chan, pw).astype(BF), chan_t) * same_y.astype(F32)).astype(BF)
    pw_bwd = (dot(dot(chan, pw).astype(BF), chan_t) * same_y.astype(F32)).astype(BF)

    def forward_middle(q):
        spec = spectrum(0, q)
        spec_in[q] = spec
        mix(1, q, expand(spec, 0, need("mask"), need("spread1")), need("sum1"))

    def forward_beside(slot):
        if slot == 0:
            need("rep")
            w_in.wait()
            wf[...] = jnp.zeros((NQ, RB, 512), F32)
            for r in range(RL):
                for m in range(ML):
                    q, row = m // MQ, (r * MQ + m % MQ) * 2
                    wf[q, row : row + 2, :400] = w_v[r * ML + m].astype(F32)
            for x in range(XL):
                base[x] = dot(pw_fwd, lbf[x]) + bias
            cot_in.wait()
            for x in range(XL):
                spread_rows(cot_v, x, cotf.at[x])
        if slot == 3:
            need("kmask")
            for q in range(NQ):
                kmask = tab["kmask"][lax.rem(gx + q, 2)]
                both = expand(spec_in[q], 4, kmask, need("spread1"))
                e00[q] = both[:RB]
                e11[q] = both[RB:]

    exchange(0, forward_middle, forward_beside)
    for x in range(XL):
        pre = base[x] + image_of(NQ - 1, x)
        delta = (cotf[x] * gelu_slope(pre)).astype(BF)
        lbf[x, :CY] = delta
        lbf[x, CY:] = delta[:48]
        if x % 2:
            zt_pair(lbf, x - 1)

    gx_send_packed(2)
    gs_out = pltpu.make_async_copy(gs_v, gs_hbm, out_sem.at[XL])

    def backward_middle(q):
        terms = expand(spectrum(2, q), 2, need("mask"), need("spread2"))
        mix(3, q, terms, need("sum2"))
        grad[q] = terms[:RB] * e00[q] + terms[RB:] * e11[q]

    def backward_beside(slot):
        if slot == 0:
            for x in range(XL):
                base[x] = dot(pw_bwd, lbf[x])
        if slot == 3:
            for r in range(RL):
                for m in range(ML):
                    q, row = m // MQ, (r * MQ + m % MQ) * 2
                    gs_v[r * ML + m] = grad[q, row : row + 2, :400]
            gs_out.start()

    exchange(2, backward_middle, backward_beside)
    zsum = need("zsum")

    def out_copy(x):
        return pltpu.make_async_copy(out_v.at[x], out_hbm.at[x], out_sem.at[x])

    for x in range(XL):
        field = base[x] + image_of(NQ - 1, x)
        out_v[x] = field.astype(BF)
        out_copy(x).start()
        zs = dot((field * gain0).astype(BF), zsum)
        acc = zs[:8]
        for c in range(1, CY // 8):
            acc = acc + zs[8 * c : 8 * c + 8]
        gp_ref[x] = (acc[:4] + acc[4:])[:, :NZ]

    gp_out = pltpu.make_async_copy(gp_ref, gp_hbm, out_sem.at[XL + 1])
    gp_out.start()
    for x in range(XL):
        out_copy(x).wait()
    gs_out.wait()
    gp_out.wait()
    for i in range(4 * NQ):
        all_blocks(gxs, gx_ss, i, GX).wait()
        all_blocks(gys, gy_ss, i, GY).wait()


def hand_over(*refs):
    given, result, held = refs[:3], refs[3:6], refs[6:9]
    rows, wide, in_sem, out_sem = refs[9:]
    ins = [pltpu.make_async_copy(given[0].at[x], rows.at[x], in_sem.at[x]) for x in range(XL)]
    outs = [
        pltpu.make_async_copy(held[0].at[:, x], result[0].at[:, x], out_sem.at[x])
        for x in range(XL)
    ]
    for a in (1, 2):
        ins.append(pltpu.make_async_copy(given[a], held[a], in_sem.at[XL + a - 1]))
        outs.append(pltpu.make_async_copy(held[a], result[a], out_sem.at[XL + a - 1]))
    for c in ins:
        c.start()
    for i, (a, b) in enumerate(zip(ins, outs)):
        a.wait()
        if i < XL:
            wide[i] = rows[i].astype(F32)
            for c in range(C):
                held[0][c, i] = wide[i, c * YL : (c + 1) * YL, :].astype(BF)
        b.start()
    for c in outs:
        c.wait()


def on_device(
    layer_input, cotangent, log_perm, well_cells, well_rates, inject_gain, spectral_weight,
    point_weight, point_bias,
):
    table = tables()
    weight = jnp.transpose(spectral_weight, (1, 2, 0, 3)).reshape(RL * ML, 2, C * C)
    hbm = pl.BlockSpec(memory_space=pl.ANY)
    scratch = [
        pltpu.VMEM((C, XL, YL, ZT), BF),
        pltpu.VMEM((C, XL, YL, ZT), BF),
        pltpu.VMEM((RL * ML, 2, C * C), BF),
        pltpu.VMEM((XL, CY, ZT), BF),
        pltpu.VMEM((RL * ML, 2, C * C), F32),
        pltpu.VMEM((XL, 128, ZT), BF),
        pltpu.VMEM((XL, CY, ZT), F32),
        pltpu.VMEM((XL, CY, ZT), F32),
        pltpu.VMEM((NQ, RB, 512), F32),
        pltpu.VMEM((XL * YL, NZ), F32),
        pltpu.VMEM((NMODE, XL, 128), F32),
        pltpu.VMEM((NMODE, XL, 128), F32),
        pltpu.VMEM((NQ, RB, 512), F32),
        pltpu.VMEM((NQ, RB, 512), F32),
        pltpu.VMEM((NQ, RB, 512), F32),
        pltpu.VMEM((NQ, QL, QL), BF),
        pltpu.VMEM((4 * NQ, GX, 16, LANES), BF),
        pltpu.VMEM((4 * NQ, GX, 16, LANES), BF),
        pltpu.VMEM((4 * NQ, GY, 8, QL), BF),
        pltpu.VMEM((4 * NQ, GY, 8, QL), BF),
        pltpu.SemaphoreType.DMA((4 * NQ,)),
        pltpu.SemaphoreType.DMA((4 * NQ,)),
        pltpu.SemaphoreType.DMA((4 * NQ,)),
        pltpu.SemaphoreType.DMA((4 * NQ,)),
        pltpu.SemaphoreType.DMA((3 + XL // 2,)),
        pltpu.SemaphoreType.DMA((len(TABLE_ORDER),)),
        pltpu.SemaphoreType.DMA((XL + 2,)),
        pltpu.VMEM((XL, YL, NZ), F32),
        pltpu.VMEM((XL, YL, NZ), F32),
        pltpu.VMEM((1, well_cells.shape[0]), jnp.int32),
        pltpu.VMEM(well_rates.shape[::-1], jnp.int32),
        pltpu.VMEM((2, C), F32),
        pltpu.VMEM((C, C), BF),
        pltpu.VMEM((1, C), F32),
        pltpu.SemaphoreType.DMA((6,)),
    ]
    for n in TABLE_ORDER:
        shape = table[n].shape[1:] if n in OWN else table[n].shape
        scratch.append(pltpu.VMEM(shape, BF))
    results = (
        jax.ShapeDtypeStruct((C, XL, YL, ZT), BF),
        jax.ShapeDtypeStruct((RL * ML, 2, C * C), F32),
        jax.ShapeDtypeStruct((XL, YL, NZ), F32),
    )
    done = pl.pallas_call(
        kernel,
        out_shape=(jax.ShapeDtypeStruct((XL, CY, ZT), BF),) + results[1:],
        in_specs=[hbm] * (9 + len(TABLE_ORDER)),
        out_specs=(hbm, hbm, hbm),
        scratch_shapes=scratch,
        compiler_params=pltpu.CompilerParams(
            collective_id=0, has_side_effects=True, vmem_limit_bytes=56 * 1024 * 1024
        ),
    )(
        layer_input, cotangent, weight, log_perm, well_cells.reshape(1, -1), well_rates.T,
        inject_gain, point_weight, point_bias.reshape(1, -1),
        *[jnp.asarray(table[n]) for n in TABLE_ORDER],
    )
    grad_input, grad_spec, grad_perm = pl.pallas_call(
        hand_over,
        out_shape=results,
        in_specs=[hbm] * 3,
        out_specs=(hbm, hbm, hbm),
        scratch_shapes=[pltpu.VMEM(r.shape, r.dtype) for r in results]
        + [
            pltpu.VMEM((XL, CY, ZT), BF),
            pltpu.VMEM((XL, CY, ZT), F32),
            pltpu.SemaphoreType.DMA((XL + 2,)),
            pltpu.SemaphoreType.DMA((XL + 2,)),
        ],
        compiler_params=pltpu.CompilerParams(vmem_limit_bytes=56 * 1024 * 1024),
    )(*done)
    grad_spec = jnp.transpose(grad_spec.reshape(RL, ML, 2, C * C), (2, 0, 1, 3))
    return grad_input, grad_spec, grad_perm


def solution(mesh):
    return jax.shard_map(
        on_device,
        mesh=mesh,
        in_specs=(
            P(None, "gx", "gy", None),
            P(None, "gx", "gy", None),
            P("gx", "gy", None),
            P(),
            P(),
            P(),
            P(None, "gy", "gx", None),
            P(),
            P(),
        ),
        out_specs=(P(None, "gx", "gy", None), P(None, "gy", "gx", None), P("gx", "gy", None)),
        check_vma=False,
    )
```

```python
import math

import jax
import jax.numpy as jnp
import ml_dtypes
import numpy as np
from jax import lax
from jax.experimental import pallas as pl
from jax.experimental.pallas import tpu as pltpu
from jax.sharding import PartitionSpec as P

C = 20
NX, NY, NZ, NT = 128, 128, 64, 16
MX, MY, MZ, MT = 24, 24, 24, 6
GX, GY = 16, 32
XL, YL = NX // GX, NY // GY
ML = MZ * MT // GX
RL = MX * MY // GY
ZT = NZ * NT
CY = C * YL
NMODE = 2 * MZ * MT
NQ = 3
MQ = ML // NQ
LANES = 256
QL = 128
RB = 128
BF = jnp.bfloat16
F32 = jnp.float32
MESH = pl.DeviceIdType.MESH
INV_ROOT_TWO = 1.0 / math.sqrt(2.0)
INV_ROOT_TWO_PI = 1.0 / math.sqrt(2.0 * math.pi)


def freq(j, n):
    return np.where(j < n // 2, j, j - n)


def lane_of(m, cy):
    if m == 0:
        return cy
    if m == 2:
        return 128 + cy
    return 80 + cy if cy < 48 else 208 + cy - 48


X_FAR = [8] + [o for k in range(7, 0, -1) for o in (k, GX - k)]
Y_FAR = sorted(
    ((dz, dx) for dz in range(8) for dx in range(4) if dz or dx),
    key=lambda d: -(min(d[0], 8 - d[0]) + min(d[1], 4 - d[1])),
)


def first_jx(d):
    return 3 * d // 4


def tables():
    jz, jt = np.divmod(np.arange(MZ * MT), MT)
    k = np.arange(ZT)
    turns = (freq(jz, MZ)[:, None] * (k // NT)[None] * NT + jt[:, None] * (k % NT)[None] * NZ) % ZT
    ang = 2 * np.pi / ZT * turns
    cos, sin = np.cos(ang) / math.sqrt(ZT), np.sin(ang) / math.sqrt(ZT)
    kap = np.where(jt == 0, 1.0, 2.0)[:, None]
    ft = np.stack([cos, -sin], 1)
    inv = np.stack([kap * cos, -kap * sin], 1)

    def by_chunk(a):
        return a.reshape(GX, NQ, MQ, 2, ZT).transpose(1, 0, 2, 3, 4).reshape(NMODE, ZT)

    ft, inv = by_chunk(ft), by_chunk(inv)
    jx = np.arange(MX)
    ang = 2 * np.pi / NX * (freq(jx, MX)[:, None] * np.arange(NX)[None] % NX)
    cx = (np.cos(ang) / math.sqrt(NX)).reshape(MX, GX, XL)
    sx = (np.sin(ang) / math.sqrt(NX)).reshape(MX, GX, XL)
    wx = np.zeros((MX, 2, GX, 2, XL))
    wx[:, 0, :, 0], wx[:, 0, :, 1] = cx, sx
    wx[:, 1, :, 1], wx[:, 1, :, 0] = cx, -sx
    wx = wx.reshape(2 * MX, 2 * NX)
    perm = np.zeros((LANES, 2 * QL))
    for m in range(MQ):
        for c in range(C):
            for y in range(YL):
                perm[lane_of(m, c * YL + y), y * 64 + m * C + c] = 1
    pick = np.zeros((GY, 2, 2, 2, 2, MX, 2))
    for d in range(GY):
        for s in range(2):
            if s == 1 and d % 4 in (0, 3):
                continue
            for y in range(2):
                for p in range(2):
                    pick[d, y, s, p, y, first_jx(d) + s, p] = 1
    pick = pick.reshape(GY * 8, MX * 4)
    wx = pick.reshape(GY * 8, 2, 2 * MX).sum(1) @ wx
    vc = np.zeros((GY, RL, 2, GY, YL, 2, 2))
    for d in range(GY):
        for i in range(RL):
            a, b = divmod(d * RL + i, MY)
            ang = 2 * np.pi / NY * (int(freq(np.array(b), MY)) * np.arange(NY) % NY)
            cy = (np.cos(ang) / math.sqrt(NY)).reshape(GY, YL)
            sy = (np.sin(ang) / math.sqrt(NY)).reshape(GY, YL)
            s = a - first_jx(d)
            vc[d, i, 0, :, :, s, 0], vc[d, i, 0, :, :, s, 1] = cy, sy
            vc[d, i, 1, :, :, s, 1], vc[d, i, 1, :, :, s, 0] = cy, -sy
    vc = vc.reshape(GY, 2 * RL, GY, 2, 2, 4).transpose(0, 4, 1, 2, 3, 5)
    vc = vc.reshape(GY, 2, 2 * RL, GY * 8)
    v_pad = np.zeros((GY, 2, 48, GY * 8))
    v_pad[:, :, : 2 * RL] = vc
    v_pad = v_pad.reshape(GY, 96, GY * 8)
    u_pad = np.zeros((GY, GY * 8, 128))
    u_pad[:, :, :96] = v_pad.transpose(0, 2, 1)
    rep = np.zeros((6, RB, 128))
    forms = [
        ((0, 1), (1, -1)),
        ((1, 1), (0, 1)),
        ((0, 1), (1, 1)),
        ((1, 1), (0, -1)),
        ((0, 1), (0, 1)),
        ((1, 1), (1, 1)),
    ]
    back = np.zeros((48, 2, RB))
    mask = np.zeros((RB, QL))
    kmask = np.zeros((2, RB, QL))
    for r in range(RL):
        for m in range(MQ):
            for p in range(2):
                row = (r * MQ + m) * 2 + p
                for f, form in enumerate(forms):
                    rep[f, row, 2 * r + form[p][0]] = form[p][1]
                back[2 * r, 0, row] = 1
                back[2 * r + 1, 1, row] = 1
                mask[row, m * C : (m + 1) * C] = 1
                for g in range(2):
                    kmask[g, row, m * C : (m + 1) * C] = 1 if (MQ * g + m) % MT == 0 else 2
    spread = np.zeros((2, QL, 512))
    for m in range(MQ):
        for c in range(C):
            for o in range(C):
                spread[0, m * C + c, c * C + o] = 1
                spread[1, m * C + o, c * C + o] = 1
    cell = np.zeros((XL, C, YL, XL, YL))
    for x in range(XL):
        for y in range(YL):
            cell[x, :, y, x, y] = 1
    cell = cell.reshape(XL * CY, XL * YL)
    chan = np.zeros((CY, C))
    chan[np.arange(CY), np.arange(CY) // YL] = 1
    chan_t = np.zeros((C, 128))
    chan_t[:, :CY] = chan.T
    same_y = np.zeros((CY, 128))
    same_y[:, :CY] = np.arange(CY)[:, None] % YL == np.arange(CY)[None] % YL
    ztrep = np.zeros((2, NZ + NT, ZT))
    ztrep[:, k // NT, k] = 1
    ztrep[:, NZ + k % NT, k] = 1
    ztrep = ztrep.reshape(2 * (NZ + NT), ZT)
    zsum = np.zeros((ZT, 128))
    zsum[k, k // NT] = 1
    out = dict(
        ft=ft, inv=inv, wx=wx, xi=wx.T, perm=perm, perm_t=perm.T,
        v=v_pad, u=u_pad, rep=rep.reshape(6 * RB, 128), back=back.reshape(48, 2 * RB),
        mask=mask, kmask=kmask, spread1=spread[0], spread2=spread[1],
        sum1=spread[1].T, sum2=spread[0].T, cell=cell, chan=chan, chan_t=chan_t,
        same_y=same_y, ztrep=ztrep, zsum=zsum,
    )
    return {n: np.ascontiguousarray(a).astype(ml_dtypes.bfloat16) for n, a in out.items()}


TABLE_ORDER = (
    "cell", "chan", "ztrep", "ft", "chan_t", "same_y", "wx", "perm", "v", "rep", "mask",
    "spread1", "sum1", "back", "u", "perm_t", "xi", "inv", "kmask", "spread2", "sum2", "zsum",
)
OWN = ("v", "u")


def dot(a, b):
    return lax.dot_general(a, b, (((1,), (0,)), ((), ())), preferred_element_type=F32)


def dot_nt(a, b):
    return lax.dot_general(a, b, (((1,), (1,)), ((), ())), preferred_element_type=F32)


def dot_tn(a, b):
    return lax.dot_general(a, b, (((0,), (0,)), ((), ())), preferred_element_type=F32)


def gelu_slope(v):
    a = jnp.abs(v) * INV_ROOT_TWO
    t = 1.0 / (1.0 + 0.3275911 * a)
    poly = t * (
        0.254829592
        + t * (-0.284496736 + t * (1.421413741 + t * (-1.453152027 + t * 1.061405429)))
    )
    e = jnp.exp(-0.5 * v * v)
    tail = 0.5 * poly * e
    return jnp.where(v >= 0, 1.0 - tail, tail) + v * e * INV_ROOT_TWO_PI


def split(a):
    hi = a.astype(BF)
    return hi, (a - hi.astype(F32)).astype(BF)


def kernel(*refs):
    names = TABLE_ORDER
    x_hbm, cot_hbm, w_hbm = refs[:3]
    small_hbm = refs[3:9]
    hbm = dict(zip(names, refs[9 : 9 + len(names)]))
    pos = 9 + len(names)
    out_hbm, gs_hbm, gp_hbm = refs[pos : pos + 3]
    pos += 3
    (
        x_v, cot_v, w_v, out_v, gs_v, lbf, base, cotf, wf, perm_s, stage, stage2, e00, e11, grad, spec_in,
        gxs, gxr, gys, gyr, gx_ss, gx_rs, gy_ss, gy_rs, in_sem, tab_sem, out_sem,
        gp_ref, perm_ref, cells_ref, rates_ref, gain_ref, pw_ref, bias_ref, small_sem,
    ) = refs[pos : pos + 35]
    small = (perm_ref, cells_ref, rates_ref, gain_ref, pw_ref, bias_ref)
    tab = dict(zip(names, refs[pos + 35 :]))
    gx = lax.axis_index("gx")
    gy = lax.axis_index("gy")

    def tab_copy(i):
        n = names[i]
        src = hbm[n]
        if n in OWN:
            src = src.at[gy]
        return pltpu.make_async_copy(src, tab[n], tab_sem.at[i])

    waited = set()

    def need(*wanted):
        for n in wanted:
            if n not in waited:
                waited.add(n)
                tab_copy(names.index(n)).wait()
        got = tuple(tab[n][...] for n in wanted)
        return got if len(got) > 1 else got[0]

    def x_in(x):
        part = pl.ds(x, 2)
        return pltpu.make_async_copy(x_hbm.at[:, part], x_v.at[:, part], in_sem.at[3 + x // 2])

    cot_in = pltpu.make_async_copy(cot_hbm, cot_v, in_sem.at[1])
    w_in = pltpu.make_async_copy(w_hbm, w_v, in_sem.at[2])
    small_in = [
        pltpu.make_async_copy(a, b, small_sem.at[i])
        for i, (a, b) in enumerate(zip(small_hbm, small))
    ]
    for c in small_in:
        c.start()
    for i in range(3):
        tab_copy(i).start()
    x_in(0).start()
    tab_copy(3).start()
    for x in range(2, XL, 2):
        x_in(x).start()
    barrier = pltpu.get_barrier_semaphore()

    @pl.loop(1, GX)
    def _(o):
        pl.semaphore_signal(
            barrier, inc=1, device_id=(lax.rem(gx + o, GX), gy), device_id_type=MESH
        )

    @pl.loop(1, GY)
    def _(o):
        pl.semaphore_signal(
            barrier, inc=1, device_id=(gx, lax.rem(gy + o, GY)), device_id_type=MESH
        )

    def gx_copy(step, q, o, landing):
        peer = lax.rem(gx + o, GX)
        return pltpu.make_async_remote_copy(
            src_ref=gxs.at[step * NQ + q, peer],
            dst_ref=gxr.at[step * NQ + q, landing],
            send_sem=gx_ss.at[step * NQ + q],
            recv_sem=gx_rs.at[step * NQ + q],
            device_id=(peer, gy),
            device_id_type=MESH,
        )

    def gy_copy(step, q, o, landing):
        peer = lax.rem(gy // 4 + o[0], 8) * 4 + lax.rem(gy + o[1], 4)
        return pltpu.make_async_remote_copy(
            src_ref=gys.at[step * NQ + q, peer],
            dst_ref=gyr.at[step * NQ + q, landing],
            send_sem=gy_ss.at[step * NQ + q],
            recv_sem=gy_rs.at[step * NQ + q],
            device_id=(gx, peer),
            device_id_type=MESH,
        )

    def all_blocks(buf, sem, i, peers):
        blocks = buf.at[i, pl.ds(0, peers - 1)]
        return pltpu.make_async_copy(blocks, blocks, sem.at[i])

    def gx_wait(step, q):
        all_blocks(gxr, gx_rs, step * NQ + q, GX).wait()

    def gy_wait(step, q):
        all_blocks(gyr, gy_rs, step * NQ + q, GY).wait()

    def gy_send(step, q):
        for o in Y_FAR:
            gy_copy(step, q, o, gy).start()
        gyr[step * NQ + q, gy] = gys[step * NQ + q, gy]

    lane = lax.broadcasted_iota(jnp.int32, (16, 128), 1)
    first_pair = lax.broadcasted_iota(jnp.int32, (GY * 8, QL), 0) % 8 < 4

    for c in small_in:
        c.wait()
    chan = need("chan")
    chan_f = chan.astype(F32)
    gain0 = jnp.sum(chan_f * gain_ref[0:1, :], axis=1, keepdims=True)
    gain1 = jnp.sum(chan_f * gain_ref[1:2, :], axis=1, keepdims=True)
    bias = jnp.sum(chan_f * bias_ref[...], axis=1, keepdims=True)

    for x in range(XL):
        perm_s[x * YL : (x + 1) * YL, :] = perm_ref[x]
    cell = need("cell")
    perm_hi, perm_lo = split(perm_s[...])
    col = lax.broadcasted_iota(jnp.int32, (XL * YL, 32), 0)
    cell_id = (gx * XL + col // YL) * NY + gy * YL + col % YL
    hits = (cells_ref[...] == cell_id).astype(BF)
    inflow = 0.5 * dot_nt(hits, rates_ref[...].astype(F32).astype(BF))
    perm_rows = dot(cell, perm_hi) + dot(cell, perm_lo)
    flow_rows = dot(cell, inflow.astype(BF))
    ztrep = need("ztrep")

    def spread_rows(src, x, dst):
        for c in range(C):
            dst[c * YL : (c + 1) * YL, :] = src[c, x].astype(F32)

    def zt_pair(field, x):
        z = dot_nt(need("ft"), field[x : x + 2].reshape(256, ZT))
        stage[:, x, :] = z[:, :128]
        stage[:, x + 1, :] = z[:, 128:]

    parts = jnp.concatenate(
        [
            jnp.concatenate([gain0] * XL, axis=0) * perm_rows,
            jnp.concatenate([gain1] * XL, axis=0) * flow_rows,
        ],
        axis=1,
    )
    parts = jnp.concatenate(split(parts), axis=1)
    for x in range(XL):
        if x % 2 == 0:
            x_in(x).wait()
        added = dot(parts[x * CY : (x + 1) * CY], ztrep)
        spread_rows(x_v, x, base.at[x])
        total = (base[x] + added).astype(BF)
        lbf[x, :CY] = total
        lbf[x, CY:] = total[:48]
        if x % 2:
            zt_pair(lbf, x - 1)
    w_in.start()
    for i in range(4, 9):
        tab_copy(i).start()
    cot_in.start()
    for i in range(9, len(names)):
        tab_copy(i).start()

    def pack(q, peer, into):
        row = (q * GX + peer) * MQ * 2
        blk = [stage[pl.ds(row + 2 * m, 2)].reshape(16, 128) for m in range(MQ)]
        into[:, :128] = jnp.where(lane < 80, blk[0], blk[1]).astype(BF)
        into[:, 128:] = jnp.where(lane < 80, blk[2], pltpu.roll(blk[1], 32, 1)).astype(BF)

    def gx_send(step, q):
        for o in X_FAR:
            gx_copy(step, q, o, gx).start()
        gxr[step * NQ + q, gx] = gxs[step * NQ + q, gx]

    def gx_send_packed(step):
        for q in range(NQ):
            for peer in range(GX):
                pack(q, peer, gxs.at[step * NQ + q, peer])
            gx_send(step, q)

    def to_owners(step, q):
        gx_wait(step, q)
        got = gxr[step * NQ + q].reshape(256, LANES)
        xs = dot(need("wx"), got).astype(BF)
        ys = dot(xs, need("perm"))
        rows = jnp.where(first_pair, ys[:, :QL], ys[:, QL:])
        gys[step * NQ + q] = rows.reshape(GY, 8, QL).astype(BF)
        gy_send(step, q)

    def gy_rows(step, q):
        gy_wait(step, q)
        return gyr[step * NQ + q].astype(F32).reshape(GY * 8, QL).astype(BF)

    def spectrum(step, q):
        both = dot(need("v"), gy_rows(step, q))
        spec = (both[:48] + pltpu.roll(both[48:], 64, 1)).astype(BF)
        return jnp.concatenate([spec, jnp.zeros((80, QL), BF)], axis=0)

    def expand(spec, forms, mask, spread):
        rep = tab["rep"][forms * RB : (forms + 2) * RB, :]
        rows = dot(rep, spec).astype(BF) * jnp.concatenate([mask, mask], axis=0)
        return dot(rows, spread)

    def mix(step, q, terms, summing):
        mask = need("mask")
        wide = jnp.concatenate([wf[q], wf[q]], axis=0)
        rows = dot((terms * wide).astype(BF), summing).astype(BF)
        rows = rows * jnp.concatenate([mask, mask], axis=0)
        mixed = dot(need("back"), rows)
        pair = jnp.concatenate([mixed, pltpu.roll(mixed, 64, 1), jnp.zeros((32, QL), F32)], axis=0)
        gys[step * NQ + q] = dot(need("u"), pair.astype(BF)).reshape(GY, 8, QL).astype(BF)
        gy_send(step, q)

    def to_columns(step, q):
        gy_wait(step, q)
        rows = gyr[step * NQ + q].astype(F32).reshape(GY * 8, QL)
        wide = jnp.concatenate(
            [jnp.where(first_pair, rows, 0.0), jnp.where(first_pair, 0.0, rows)], axis=1
        )
        xs = dot(wide.astype(BF), need("perm_t")).astype(BF)
        gxs[step * NQ + q] = dot(need("xi"), xs).astype(BF).reshape(GX, 16, LANES)
        gx_send(step, q)

    def unpack(step, q, src):
        got = [
            gxr[step * NQ + q, src, :, t * 128 : (t + 1) * 128].astype(F32) for t in range(2)
        ]
        middle = jnp.where(lane < 48, pltpu.roll(got[0], 48, 1), pltpu.roll(got[1], 96, 1))
        row = (q * GX + src) * MQ * 2
        for m, v in enumerate((got[0], middle, got[1])):
            stage2[row + 2 * m : row + 2 * m + 2] = v.reshape(2, 8, 128)

    def receive_images(step, q):
        gx_wait(step, q)
        for src in range(GX):
            unpack(step, q, src)

    def image_of(q, x):
        rows = slice(q * 2 * ML * GX // NQ, (q + 1) * 2 * ML * GX // NQ)
        return dot_tn(stage2[rows, x, :].astype(BF), need("inv")[rows])[:CY]

    def exchange(step, middle, beside):
        beside(0)
        for q in range(NQ):
            to_owners(step, q)
        beside(1)
        for q in range(NQ):
            middle(q)
        beside(2)
        for q in range(NQ):
            to_columns(step + 1, q)
        beside(3)
        for q in range(NQ):
            receive_images(step + 1, q)
            if q < NQ - 1:
                for x in range(XL):
                    base[x] += image_of(q, x)

    pl.semaphore_wait(barrier, GX + GY - 2)
    gx_send_packed(0)

    chan_t, same_y = need("chan_t", "same_y")
    pw = pw_ref[...]
    pw_fwd = (dot(dot_nt(chan, pw).astype(BF), chan_t) * same_y.astype(F32)).astype(BF)
    pw_bwd = (dot(dot(chan, pw).astype(BF), chan_t) * same_y.astype(F32)).astype(BF)

    def forward_middle(q):
        spec = spectrum(0, q)
        spec_in[q] = spec
        mix(1, q, expand(spec, 0, need("mask"), need("spread1")), need("sum1"))

    def forward_beside(slot):
        if slot == 0:
            need("rep")
            w_in.wait()
            wf[...] = jnp.zeros((NQ, RB, 512), F32)
            for r in range(RL):
                for m in range(ML):
                    q, row = m // MQ, (r * MQ + m % MQ) * 2
                    wf[q, row : row + 2, :400] = w_v[r * ML + m].astype(F32)
            for x in range(XL):
                base[x] = dot(pw_fwd, lbf[x]) + bias
            cot_in.wait()
            for x in range(XL):
                spread_rows(cot_v, x, cotf.at[x])
        if slot == 3:
            need("kmask")
            for q in range(NQ):
                kmask = tab["kmask"][lax.rem(gx + q, 2)]
                both = expand(spec_in[q], 4, kmask, need("spread1"))
                e00[q] = both[:RB]
                e11[q] = both[RB:]

    exchange(0, forward_middle, forward_beside)
    for x in range(XL):
        pre = base[x] + image_of(NQ - 1, x)
        delta = (cotf[x] * gelu_slope(pre)).astype(BF)
        lbf[x, :CY] = delta
        lbf[x, CY:] = delta[:48]
        if x % 2:
            zt_pair(lbf, x - 1)

    gx_send_packed(2)
    gs_out = pltpu.make_async_copy(gs_v, gs_hbm, out_sem.at[XL])

    def backward_middle(q):
        terms = expand(spectrum(2, q), 2, need("mask"), need("spread2"))
        mix(3, q, terms, need("sum2"))
        grad[q] = terms[:RB] * e00[q] + terms[RB:] * e11[q]

    def backward_beside(slot):
        if slot == 0:
            for x in range(XL):
                base[x] = dot(pw_bwd, lbf[x])
        if slot == 3:
            for r in range(RL):
                for m in range(ML):
                    q, row = m // MQ, (r * MQ + m % MQ) * 2
                    gs_v[r * ML + m] = grad[q, row : row + 2, :400]
            gs_out.start()

    exchange(2, backward_middle, backward_beside)
    zsum = need("zsum")

    def out_copy(x):
        return pltpu.make_async_copy(out_v.at[x], out_hbm.at[x], out_sem.at[x])

    for x in range(XL):
        field = base[x] + image_of(NQ - 1, x)
        out_v[x] = field.astype(BF)
        out_copy(x).start()
        zs = dot((field * gain0).astype(BF), zsum)
        acc = zs[:8]
        for c in range(1, CY // 8):
            acc = acc + zs[8 * c : 8 * c + 8]
        gp_ref[x] = (acc[:4] + acc[4:])[:, :NZ]

    gp_out = pltpu.make_async_copy(gp_ref, gp_hbm, out_sem.at[XL + 1])
    gp_out.start()
    for x in range(XL):
        out_copy(x).wait()
    gs_out.wait()
    gp_out.wait()
    for i in range(4 * NQ):
        all_blocks(gxs, gx_ss, i, GX).wait()
        all_blocks(gys, gy_ss, i, GY).wait()


def hand_over(*refs):
    given, result, held = refs[:3], refs[3:6], refs[6:9]
    rows, wide, in_sem, out_sem = refs[9:]
    ins = [pltpu.make_async_copy(given[0].at[x], rows.at[x], in_sem.at[x]) for x in range(XL)]
    outs = [
        pltpu.make_async_copy(held[0].at[:, x], result[0].at[:, x], out_sem.at[x])
        for x in range(XL)
    ]
    for a in (1, 2):
        ins.append(pltpu.make_async_copy(given[a], held[a], in_sem.at[XL + a - 1]))
        outs.append(pltpu.make_async_copy(held[a], result[a], out_sem.at[XL + a - 1]))
    for c in ins:
        c.start()
    for i, (a, b) in enumerate(zip(ins, outs)):
        a.wait()
        if i < XL:
            wide[i] = rows[i].astype(F32)
            for c in range(C):
                held[0][c, i] = wide[i, c * YL : (c + 1) * YL, :].astype(BF)
        b.start()
    for c in outs:
        c.wait()


def on_device(
    layer_input, cotangent, log_perm, well_cells, well_rates, inject_gain, spectral_weight,
    point_weight, point_bias,
):
    table = tables()
    weight = jnp.transpose(spectral_weight, (1, 2, 0, 3)).reshape(RL * ML, 2, C * C)
    hbm = pl.BlockSpec(memory_space=pl.ANY)
    scratch = [
        pltpu.VMEM((C, XL, YL, ZT), BF),
        pltpu.VMEM((C, XL, YL, ZT), BF),
        pltpu.VMEM((RL * ML, 2, C * C), BF),
        pltpu.VMEM((XL, CY, ZT), BF),
        pltpu.VMEM((RL * ML, 2, C * C), F32),
        pltpu.VMEM((XL, 128, ZT), BF),
        pltpu.VMEM((XL, CY, ZT), F32),
        pltpu.VMEM((XL, CY, ZT), F32),
        pltpu.VMEM((NQ, RB, 512), F32),
        pltpu.VMEM((XL * YL, NZ), F32),
        pltpu.VMEM((NMODE, XL, 128), F32),
        pltpu.VMEM((NMODE, XL, 128), F32),
        pltpu.VMEM((NQ, RB, 512), F32),
        pltpu.VMEM((NQ, RB, 512), F32),
        pltpu.VMEM((NQ, RB, 512), F32),
        pltpu.VMEM((NQ, QL, QL), BF),
        pltpu.VMEM((4 * NQ, GX, 16, LANES), BF),
        pltpu.VMEM((4 * NQ, GX, 16, LANES), BF),
        pltpu.VMEM((4 * NQ, GY, 8, QL), BF),
        pltpu.VMEM((4 * NQ, GY, 8, QL), BF),
        pltpu.SemaphoreType.DMA((4 * NQ,)),
        pltpu.SemaphoreType.DMA((4 * NQ,)),
        pltpu.SemaphoreType.DMA((4 * NQ,)),
        pltpu.SemaphoreType.DMA((4 * NQ,)),
        pltpu.SemaphoreType.DMA((3 + XL // 2,)),
        pltpu.SemaphoreType.DMA((len(TABLE_ORDER),)),
        pltpu.SemaphoreType.DMA((XL + 2,)),
        pltpu.VMEM((XL, YL, NZ), F32),
        pltpu.VMEM((XL, YL, NZ), F32),
        pltpu.VMEM((1, well_cells.shape[0]), jnp.int32),
        pltpu.VMEM(well_rates.shape[::-1], jnp.int32),
        pltpu.VMEM((2, C), F32),
        pltpu.VMEM((C, C), BF),
        pltpu.VMEM((1, C), F32),
        pltpu.SemaphoreType.DMA((6,)),
    ]
    for n in TABLE_ORDER:
        shape = table[n].shape[1:] if n in OWN else table[n].shape
        scratch.append(pltpu.VMEM(shape, BF))
    results = (
        jax.ShapeDtypeStruct((C, XL, YL, ZT), BF),
        jax.ShapeDtypeStruct((RL * ML, 2, C * C), F32),
        jax.ShapeDtypeStruct((XL, YL, NZ), F32),
    )
    done = pl.pallas_call(
        kernel,
        out_shape=(jax.ShapeDtypeStruct((XL, CY, ZT), BF),) + results[1:],
        in_specs=[hbm] * (9 + len(TABLE_ORDER)),
        out_specs=(hbm, hbm, hbm),
        scratch_shapes=scratch,
        compiler_params=pltpu.CompilerParams(
            collective_id=0, has_side_effects=True, vmem_limit_bytes=56 * 1024 * 1024
        ),
    )(
        layer_input, cotangent, weight, log_perm, well_cells.reshape(1, -1), well_rates.T,
        inject_gain, point_weight, point_bias.reshape(1, -1),
        *[jnp.asarray(table[n]) for n in TABLE_ORDER],
    )
    grad_input, grad_spec, grad_perm = pl.pallas_call(
        hand_over,
        out_shape=results,
        in_specs=[hbm] * 3,
        out_specs=(hbm, hbm, hbm),
        scratch_shapes=[pltpu.VMEM(r.shape, r.dtype) for r in results]
        + [
            pltpu.VMEM((XL, CY, ZT), BF),
            pltpu.VMEM((XL, CY, ZT), F32),
            pltpu.SemaphoreType.DMA((XL + 2,)),
            pltpu.SemaphoreType.DMA((XL + 2,)),
        ],
        compiler_params=pltpu.CompilerParams(vmem_limit_bytes=56 * 1024 * 1024),
    )(*done)
    grad_spec = jnp.transpose(grad_spec.reshape(RL, ML, 2, C * C), (2, 0, 1, 3))
    return grad_input, grad_spec, grad_perm


def solution(mesh):
    return jax.shard_map(
        on_device,
        mesh=mesh,
        in_specs=(
            P(None, "gx", "gy", None),
            P(None, "gx", "gy", None),
            P("gx", "gy", None),
            P(),
            P(),
            P(),
            P(None, "gy", "gx", None),
            P(),
            P(),
        ),
        out_specs=(P(None, "gx", "gy", None), P(None, "gy", "gx", None), P("gx", "gy", None)),
        check_vma=False,
    )
```
